1024 devices in a mesh: dp: 128 (over y, z_hi, x, core), tensor: 8 (over z_lo).
Axes of the slice: x: 4, y: 8, z: 16 (z_hi: 2, z_lo: 8; z = z_hi * 8 + z_lo), core: 2. Of those that a mesh axis runs over, the one named last changes fastest.
Arguments:
- cache_keys: bfloat16 [512, 1536, 1024], P('dp', None, 'tensor'), may hold values from -6 to 6
- cache_values: bfloat16 [512, 1536, 1024], P('dp', None, 'tensor'), may hold values from -6 to 6
- lengths: int32 [512], P('dp'), may hold values from 1 to 3, as said below
- finished: int32 [512], P('dp'), may hold values from 0 to 1, as said below
- migrations: int32 [64, 4], replicated, may hold values from 0 to 127, as said below
- queries: bfloat16 [8, 512, 8192], P(None, 'dp', 'tensor'), may hold values from -6 to 6
- new_keys: bfloat16 [8, 512, 1024], P(None, 'dp', 'tensor'), may hold values from -6 to 6
- new_values: bfloat16 [8, 512, 1024], P(None, 'dp', 'tensor'), may hold values from -6 to 6
- out_weight: bfloat16 [8192, 2560], P('tensor'), may hold values from -0.5 to 0.5
Outputs:
- output: bfloat16 [8, 512, 2560], P(None, 'dp')
The draws below stay inside these ranges and needn't reach their ends.
Inputs may be any that keep to these rules, and one draw needn't show every extreme that they name: `lengths`: whole blocks of 512 tokens; some row holds 3 blocks in every draw. `finished`: 1 marks a row whose generation has ended; its slot is free. `migrations`: each entry moves one row to the next group, (source + 1) modulo the number of groups. No group is a source twice or a destination twice, and no group is both. The moved row is unfinished and the destination slot is finished.
All inputs are finite; a program needn't handle non-finite values.
Results may differ from the reference program's by a relative error of at most 0.0054.
Values may be sent and summed in bfloat16 or wider, within the bound.
A program may use at most 32 MiB of HBM per device.

```python
import jax
import jax.numpy as jnp
from jax import lax

HQ = 64
KVH = 8
HD = 128
DOUT = 2560
BLOCK = 512
STEPS = 8
ROWS_DEV = 4
MAXB = 3
ROWS = 512
MIGS = 64
CACHE = 1536
N_DP = 128


def plan(key):
    order_keys = jax.random.split(jax.random.fold_in(key, 21), N_DP)
    slot_orders = jax.vmap(lambda sub_key: jax.random.permutation(sub_key, ROWS_DEV))(order_keys).astype(jnp.int32)
    offset = jax.random.randint(jax.random.fold_in(key, 22), (), 0, 2)
    chosen = (2 * jnp.arange(MIGS) + offset).astype(jnp.int32)
    target = ((chosen + 1) % N_DP).astype(jnp.int32)
    entries = jnp.stack([chosen, target, slot_orders[chosen, 0], slot_orders[target, 1]], axis=1)
    is_target = jnp.zeros((N_DP,), jnp.int32).at[target].set(1)[:, None]
    busy_extra = (jax.random.randint(jax.random.fold_in(key, 23), (N_DP, ROWS_DEV), 0, 4) == 0).astype(jnp.int32)
    spare_first = jax.random.randint(jax.random.fold_in(key, 24), (N_DP, 1), 0, 2)
    rank_ids = jnp.arange(ROWS_DEV)[None, :]
    busy_rank = jnp.where(rank_ids == 0, 0, busy_extra)
    spare_rank = jnp.where(rank_ids == 0, spare_first, 1)
    status_rank = jnp.where(is_target == 1, spare_rank, busy_rank).astype(jnp.int32)
    group_ids = jnp.broadcast_to(jnp.arange(N_DP)[:, None], (N_DP, ROWS_DEV))
    finished = jnp.zeros((N_DP, ROWS_DEV), jnp.int32).at[group_ids, slot_orders].set(status_rank)
    return (entries.astype(jnp.int32), finished.reshape(ROWS).astype(jnp.int32))


def draw_migrations(key, part):
    entries, status = plan(key)
    return entries


def draw_finished(key, part):
    entries, status = plan(key)
    return status


def draw_lengths(key, part):
    key = jax.random.fold_in(key, 11)
    group_level = jax.random.randint(jax.random.fold_in(key, 1), (N_DP, 1), 1, MAXB + 1)
    row_blocks = jax.random.randint(jax.random.fold_in(key, 2), (N_DP, ROWS_DEV), 1, group_level + 1).reshape(ROWS)
    forced_row = jax.random.randint(jax.random.fold_in(key, 3), (), 0, ROWS)
    return row_blocks.at[forced_row].set(MAXB).astype(jnp.int32)


def draw_queries(key, part):
    key = jax.random.fold_in(key, 5)
    result = jnp.clip(jax.random.normal(key, (STEPS, ROWS, HQ * HD), jnp.float32), -6.0, 6.0)
    return result.astype(jnp.bfloat16)


def draw_new_keys(key, part):
    key = jax.random.fold_in(key, 6)
    result = jnp.clip(2.0 * jax.random.normal(key, (STEPS, ROWS, KVH * HD), jnp.float32), -6.0, 6.0)
    return result.astype(jnp.bfloat16)


def block_scale(rng, dims, pieces, smallest, top_value):
    def one(position, shards_of):
        heights = jax.random.uniform(jax.random.fold_in(jax.random.fold_in(rng, 6), position), (shards_of,), jnp.float32, smallest / len(pieces), top_value / len(pieces))
        return jnp.repeat(jnp.exp(heights), dims[position] // shards_of).reshape((-1,) + (1,) * (len(dims) - position - 1))

    gain = one(*pieces[0])
    for cut in pieces[1:]:
        gain = gain * one(*cut)
    return gain


def bell_draw(own_key, extent, spread, reach, shards=(), held_as=jnp.bfloat16):
    level = block_scale(own_key, extent, shards, -0.22, 0.18) if shards else 1.0
    values = jax.random.normal(own_key, extent, jnp.float32) * spread * level
    return jnp.minimum(jnp.maximum(values, -reach), reach).astype(held_as)


def setup_inputs(seed: int = 0) -> dict:
    key_of = jax.random.split(jax.random.key(seed), 10)
    return {
        "cache_keys": bell_draw(key_of[0], (ROWS, CACHE, KVH * HD), 1.0, 6.0, ((0, 128), (2, 8))),
        "cache_values": bell_draw(key_of[1], (ROWS, CACHE, KVH * HD), 1.0, 6.0, ((0, 128), (2, 8))),
        "lengths": draw_lengths(jax.random.fold_in(key_of[9], 71), 0),
        "finished": draw_finished(jax.random.fold_in(key_of[9], 71), 0),
        "migrations": draw_migrations(jax.random.fold_in(key_of[9], 71), 0),
        "queries": draw_queries(jax.random.fold_in(key_of[9], 71), 0),
        "new_keys": draw_new_keys(jax.random.fold_in(key_of[9], 71), 0),
        "new_values": bell_draw(key_of[7], (STEPS, ROWS, KVH * HD), 1.0, 6.0, ((1, 128), (2, 8))),
        "out_weight": bell_draw(key_of[8], (HQ * HD, DOUT), (HQ * HD // 64) ** -0.5, 0.5, ((0, 8),)),
    }


def slot_root(finished, migrations):
    source = migrations[:, 0] * ROWS_DEV + migrations[:, 2]
    target = migrations[:, 1] * ROWS_DEV + migrations[:, 3]
    slot_ids = jnp.arange(ROWS, dtype=jnp.int32)
    root = jnp.where(finished == 0, slot_ids, -1).astype(jnp.int32)
    root = root.at[source].set(-1)
    root = root.at[target].set(source.astype(jnp.int32))
    return root


def attend_slot(key_row, value_row, blocks, query, fresh_keys, fresh_values):
    grouping = HQ // KVH
    score_scale = 1.0 / (HD ** 0.5)
    query_heads = query.astype(jnp.float32).reshape(STEPS, KVH, grouping, HD)
    key_heads = key_row.astype(jnp.float32).reshape(CACHE, KVH, HD)
    value_heads = value_row.astype(jnp.float32).reshape(CACHE, KVH, HD)
    fresh_key_heads = fresh_keys.astype(jnp.float32).reshape(STEPS, KVH, HD)
    fresh_value_heads = fresh_values.astype(jnp.float32).reshape(STEPS, KVH, HD)
    cached_scores = jnp.einsum("skgd,ckd->skgc", query_heads, key_heads) * score_scale
    fresh_scores = jnp.einsum("skgd,ukd->skgu", query_heads, fresh_key_heads) * score_scale
    cache_mask = (jnp.arange(CACHE, dtype=jnp.int32) < blocks * BLOCK)[None, None, None, :]
    step_ids = jnp.arange(STEPS, dtype=jnp.int32)
    fresh_mask = (step_ids[None, :] <= step_ids[:, None])[:, None, None, :]
    cached_scores = jnp.where(cache_mask, cached_scores, -1e30)
    fresh_scores = jnp.where(fresh_mask, fresh_scores, -1e30)
    peak_score = jnp.maximum(jnp.max(cached_scores, axis=3), jnp.max(fresh_scores, axis=3))[..., None]
    cached_weights = jnp.exp(cached_scores - peak_score)
    fresh_weights = jnp.exp(fresh_scores - peak_score)
    totals = jnp.sum(cached_weights, axis=3) + jnp.sum(fresh_weights, axis=3)
    cached_rounded = lax.optimization_barrier(cached_weights.astype(jnp.bfloat16)).astype(jnp.float32)
    fresh_rounded = lax.optimization_barrier(fresh_weights.astype(jnp.bfloat16)).astype(jnp.float32)
    mixed_out = jnp.einsum("skgc,ckd->skgd", cached_rounded, value_heads)
    mixed_out = mixed_out + jnp.einsum("skgu,ukd->skgd", fresh_rounded, fresh_value_heads)
    return (mixed_out / totals[..., None]).astype(jnp.bfloat16).reshape(STEPS, HQ * HD)


def reference(cache_keys, cache_values, lengths, finished, migrations, queries, new_keys, new_values, out_weight):
    root = slot_root(finished, migrations)
    live_slot = root >= 0
    source_row = jnp.maximum(root, 0)

    def per_slot(slot_id):
        picked = source_row[slot_id]
        return attend_slot(cache_keys[picked], cache_values[picked], lengths[picked], queries[:, slot_id], new_keys[:, slot_id], new_values[:, slot_id])

    attended = lax.map(per_slot, jnp.arange(ROWS, dtype=jnp.int32))
    attended = jnp.where(live_slot[:, None, None], attended, jnp.zeros_like(attended))
    attended = jnp.transpose(attended, (1, 0, 2)).reshape(STEPS * ROWS, HQ * HD)
    output = jnp.dot(attended, out_weight, preferred_element_type=jnp.float32)
    return output.astype(jnp.bfloat16).reshape(STEPS, ROWS, DOUT)
```

```python
import functools

import jax
import jax.numpy as jnp
from jax import lax
from jax.experimental import pallas as pl
from jax.experimental.pallas import tpu as pltpu
from jax.sharding import PartitionSpec as P

HD = 128
BLOCK = 512
LANES = 128
MESH = pl.DeviceIdType.MESH
F32 = jnp.float32
BF16 = jnp.bfloat16


def one_hot(mask):
    return jnp.where(mask, 1.0, 0.0).astype(BF16)


def grid_ids(shape):
    return (
        lax.broadcasted_iota(jnp.int32, shape, 0),
        lax.broadcasted_iota(jnp.int32, shape, 1),
    )


def dot(a, b):
    return lax.dot_general(a, b, (((1,), (0,)), ((), ())), preferred_element_type=F32)


def dot_t(a, b):
    return lax.dot_general(a, b, (((1,), (1,)), ((), ())), preferred_element_type=F32)


def stack_heads(rows, heads):
    return jnp.concatenate([rows[:, h * HD : (h + 1) * HD] for h in range(heads)], axis=0)


def attend(query, keys, values, fresh_keys, fresh_values, limit, steps, heads):
    scale = 1.0 / HD**0.5
    scores = dot_t(query, keys) * scale
    fresh = dot_t(query, fresh_keys) * scale
    _, position = grid_ids(scores.shape)
    scores = jnp.where(position < limit, scores, -1e30)
    row, token = grid_ids(fresh.shape)
    fresh = jnp.where(token <= lax.rem(row, steps), fresh, -1e30)
    peak = jnp.maximum(
        jnp.max(scores, axis=1, keepdims=True), jnp.max(fresh, axis=1, keepdims=True)
    )
    weights = jnp.exp(scores - peak)
    fresh_weights = jnp.exp(fresh - peak)
    total = jnp.sum(weights, axis=1, keepdims=True) + jnp.sum(fresh_weights, axis=1, keepdims=True)
    mixed = dot(weights.astype(BF16), values) + dot(fresh_weights.astype(BF16), fresh_values)
    mixed = mixed / total
    return jnp.concatenate([mixed[h * steps : (h + 1) * steps] for h in range(heads)], axis=1)


def kernel(
    lengths, finished, mig, query, fresh, keys_hbm, values_hbm, weight_hbm,
    out,
    keys, values, weight, ask, asked, part, reduced, moved_part, moved_in, chunk, gathered,
    load_sem, ask_send, ask_recv, rs_send, rs_recv, mv_send, mv_recv, ag_send, ag_recv,
    *, slots, steps, heads, n_dp, n_t,
):
    g, t = lax.axis_index("dp"), lax.axis_index("tensor")
    up, down = lax.rem(g + 1, n_dp), lax.rem(g + n_dp - 1, n_dp)
    rows = slots * steps

    barrier = pltpu.get_barrier_semaphore()
    for p in range(1, n_t):
        pl.semaphore_signal(barrier, inc=1, device_id=(g, lax.rem(t + p, n_t)), device_id_type=MESH)
    for p in range(n_t):
        other = lax.rem(t + p, n_t)
        pl.semaphore_signal(barrier, inc=1, device_id=(up, other), device_id_type=MESH)
        pl.semaphore_signal(barrier, inc=1, device_id=(down, other), device_id_type=MESH)

    loads = [
        pltpu.make_async_copy(src, dst, load_sem.at[i])
        for i, (src, dst) in enumerate(
            [(keys_hbm, keys), (values_hbm, values), (weight_hbm, weight)]
        )
    ]
    for load in loads:
        load.start()

    sending = mig[0:1, :] == g
    arriving = mig[1:2, :] == g
    has_send = jnp.sum(sending.astype(jnp.int32)) > 0
    has_arrival = jnp.sum(arriving.astype(jnp.int32)) > 0
    sent_row = jnp.sum(jnp.where(sending, mig[2:3, :], 0))
    arrival_slot = jnp.sum(jnp.where(arriving, mig[3:4, :], 0))

    i, j = grid_ids((rows + steps, rows))
    slot = jnp.where(i < rows, i // steps, arrival_slot)
    order = one_hot(j == lax.rem(i, steps) * slots + slot)
    by_slot = dot(order, query[...])
    fresh_by_slot = dot(order, fresh[...])
    ask[0 : heads * steps, :] = stack_heads(by_slot[rows:], heads).astype(BF16)
    ask[heads * steps :, :] = stack_heads(fresh_by_slot[rows:], 2).astype(BF16)

    zeros = jnp.zeros((16 - steps, HD), F32)

    def pad(x):
        return jnp.concatenate([x, zeros], axis=0).astype(BF16)

    loads[0].wait()
    loads[1].wait()
    attended = []
    for r in range(slots):
        mine = slice(r * steps, (r + 1) * steps)
        mixed = attend(
            stack_heads(by_slot[mine], heads).astype(BF16),
            keys[r], values[r],
            pad(fresh_by_slot[mine, :HD]), pad(fresh_by_slot[mine, HD:]),
            lengths[r] * BLOCK, steps, heads,
        )
        stays = jnp.logical_and(
            finished[r] == 0, jnp.logical_not(jnp.logical_and(has_send, sent_row == r))
        )
        attended.append(jnp.where(stays, mixed, 0.0))
    attended = jnp.concatenate(attended, axis=0).astype(BF16)
    i, j = grid_ids((rows, rows))
    to_steps = one_hot(j == lax.rem(i, slots) * steps + i // slots)
    attended = dot(to_steps, attended).astype(BF16)

    loads[2].wait()
    half = rows // 2
    for c in range(10):
        block = dot(attended, weight[:, 256 * c : 256 * (c + 1)]).astype(BF16)
        for k in range(2):
            for h in range(2):
                piece = block[h * half : (h + 1) * half, k * LANES : (k + 1) * LANES]
                if c < 8:
                    part[c, 2 * k + h] = piece
                else:
                    part[2 * (2 * (c - 8) + k) + h, 4] = piece

    pl.semaphore_wait(barrier, 3 * n_t - 1)
    ask_copy = pltpu.make_async_remote_copy(
        ask, asked, ask_send, ask_recv, device_id=(down, t), device_id_type=MESH
    )
    ask_copy.start()

    def rs_copy(j, slot):
        return pltpu.make_async_remote_copy(
            part.at[j], reduced.at[slot], rs_send.at[j], rs_recv.at[slot],
            device_id=(g, j), device_id_type=MESH,
        )

    peers = [lax.rem(t + p, n_t) for p in range(1, n_t)]
    for j in peers:
        rs_copy(j, t).start()

    ask_copy.wait_recv()
    asked_fresh = asked[heads * steps :, :].astype(F32)
    moved = attend(
        asked[0 : heads * steps, :],
        keys[sent_row], values[sent_row],
        pad(asked_fresh[:steps]), pad(asked_fresh[steps:]),
        lengths[sent_row] * BLOCK, steps, heads,
    )
    moved = jnp.where(has_send, moved, 0.0).astype(BF16)
    for c in range(10):
        block = dot(moved, weight[:, 256 * c : 256 * (c + 1)])
        piece = jnp.concatenate([block[:, :LANES], block[:, LANES:]], axis=0).astype(BF16)
        if c < 8:
            moved_part[c, 0] = piece
        else:
            for j in range(4):
                moved_part[4 * (c - 8) + j, 1] = piece

    def mv_copy(group, j, slot):
        return pltpu.make_async_remote_copy(
            moved_part.at[j], moved_in.at[slot], mv_send.at[j], mv_recv.at[slot],
            device_id=(group, j), device_id_type=MESH,
        )

    for p in range(n_t):
        mv_copy(up, lax.rem(t + p, n_t), t).start()

    total = part[t].astype(F32)
    for j in peers:
        rs_copy(j, j).wait_recv()
        total = total + reduced[j].astype(F32)
    arrived = None
    for p in range(n_t):
        j = lax.rem(t + p, n_t)
        mv_copy(up, j, j).wait_recv()
        piece = moved_in[j].astype(F32)
        arrived = piece if arrived is None else arrived + piece
    arrived = jnp.where(has_arrival, arrived, 0.0).astype(BF16)
    i, j = grid_ids((rows, steps))
    place = one_hot(jnp.logical_and(lax.rem(i, slots) == arrival_slot, i // slots == j))
    lo = dot(place, arrived[0, :steps])
    hi = dot(place, arrived[0, steps:])
    extra = dot(place, jnp.where(lax.rem(t // 2, 2) == 0, arrived[1, :steps], arrived[1, steps:]))
    extra = jnp.where(lax.rem(t, 2) == 0, extra[:half], extra[half:])
    chunk[0] = (total[0] + lo[:half]).astype(BF16)
    chunk[1] = (total[1] + lo[half:]).astype(BF16)
    chunk[2] = (total[2] + hi[:half]).astype(BF16)
    chunk[3] = (total[3] + hi[half:]).astype(BF16)
    chunk[4] = (total[4] + extra).astype(BF16)

    def ag_copy(j, slot):
        return pltpu.make_async_remote_copy(
            chunk, gathered.at[slot], ag_send.at[j], ag_recv.at[slot],
            device_id=(g, j), device_id_type=MESH,
        )

    for j in peers:
        ag_copy(j, t).start()
    gathered[t] = chunk[...]
    for j in peers:
        ag_copy(j, j).wait_recv()
    for j in range(n_t):
        for k in range(2):
            for h in range(2):
                out[h * half : (h + 1) * half, (2 * j + k) * LANES : (2 * j + k + 1) * LANES] = (
                    gathered[j, 2 * k + h]
                )
        tile = 2 * n_t + j // 2
        h = j % 2
        out[h * half : (h + 1) * half, tile * LANES : (tile + 1) * LANES] = gathered[j, 4]

    ask_copy.wait_send()
    for j in peers:
        rs_copy(j, t).wait_send()
        ag_copy(j, t).wait_send()
    for j in range(n_t):
        mv_copy(up, j, t).wait_send()


def per_device(n_dp, n_t, cache_keys, cache_values, lengths, finished, migrations, queries,
               new_keys, new_values, out_weight):
    steps, slots, width = queries.shape
    cache = cache_keys.shape[1]
    features = out_weight.shape[1]
    heads = width // HD
    rows = steps * slots
    fresh = jnp.concatenate([new_keys, new_values], axis=2).reshape(rows, 2 * HD)
    vmem = pl.BlockSpec(memory_space=pltpu.VMEM)
    smem = pl.BlockSpec(memory_space=pltpu.SMEM)
    anywhere = pl.BlockSpec(memory_space=pl.ANY)
    dma = pltpu.SemaphoreType.DMA
    result = pl.pallas_call(
        functools.partial(kernel, slots=slots, steps=steps, heads=heads, n_dp=n_dp, n_t=n_t),
        out_shape=jax.ShapeDtypeStruct((rows, features), BF16),
        in_specs=[smem, smem, vmem, vmem, vmem, anywhere, anywhere, anywhere],
        out_specs=vmem,
        scratch_shapes=[
            pltpu.VMEM((slots, cache, HD), BF16),
            pltpu.VMEM((slots, cache, HD), BF16),
            pltpu.VMEM((width, features), BF16),
            pltpu.VMEM(((heads + 2) * steps, HD), BF16),
            pltpu.VMEM(((heads + 2) * steps, HD), BF16),
            pltpu.VMEM((n_t, 5, rows // 2, LANES), BF16),
            pltpu.VMEM((n_t, 5, rows // 2, LANES), BF16),
            pltpu.VMEM((n_t, 2, 2 * steps, LANES), BF16),
            pltpu.VMEM((n_t, 2, 2 * steps, LANES), BF16),
            pltpu.VMEM((5, rows // 2, LANES), BF16),
            pltpu.VMEM((n_t, 5, rows // 2, LANES), BF16),
            dma((3,)), dma, dma, dma((n_t,)), dma((n_t,)), dma((n_t,)), dma((n_t,)),
            dma((n_t,)), dma((n_t,)),
        ],
        compiler_params=pltpu.CompilerParams(
            collective_id=0, has_side_effects=True, vmem_limit_bytes=48 << 20
        ),
    )(
        lengths, finished, migrations.T, queries.reshape(rows, width), fresh,
        cache_keys, cache_values, out_weight,
    )
    return result.reshape(steps, slots, features)


def solution(mesh):
    sizes = dict(zip(mesh.axis_names, mesh.devices.shape))
    return jax.shard_map(
        functools.partial(per_device, sizes["dp"], sizes["tensor"]),
        mesh=mesh,
        in_specs=(
            P("dp", None, "tensor"),
            P("dp", None, "tensor"),
            P("dp"),
            P("dp"),
            P(),
            P(None, "dp", "tensor"),
            P(None, "dp", "tensor"),
            P(None, "dp", "tensor"),
            P("tensor", None),
        ),
        out_specs=P(None, "dp", None),
        check_vma=False,
    )
```

```python
import functools

import jax
import jax.numpy as jnp
from jax import lax
from jax.experimental import pallas as pl
from jax.experimental.pallas import tpu as pltpu
from jax.sharding import PartitionSpec as P

HD = 128
BLOCK = 512
LANES = 128
MESH = pl.DeviceIdType.MESH
F32 = jnp.float32
BF16 = jnp.bfloat16


def one_hot(mask):
    return jnp.where(mask, 1.0, 0.0).astype(BF16)


def grid_ids(shape):
    return (
        lax.broadcasted_iota(jnp.int32, shape, 0),
        lax.broadcasted_iota(jnp.int32, shape, 1),
    )


def dot(a, b):
    return lax.dot_general(a, b, (((1,), (0,)), ((), ())), preferred_element_type=F32)


def dot_t(a, b):
    return lax.dot_general(a, b, (((1,), (1,)), ((), ())), preferred_element_type=F32)


def stack_heads(rows, heads):
    return jnp.concatenate([rows[:, h * HD : (h + 1) * HD] for h in range(heads)], axis=0)


def attend(query, keys, values, fresh_keys, fresh_values, limit, steps, heads):
    scale = 1.0 / HD**0.5
    scores = dot_t(query, keys) * scale
    fresh = dot_t(query, fresh_keys) * scale
    _, position = grid_ids(scores.shape)
    scores = jnp.where(position < limit, scores, -1e30)
    row, token = grid_ids(fresh.shape)
    fresh = jnp.where(token <= lax.rem(row, steps), fresh, -1e30)
    peak = jnp.maximum(
        jnp.max(scores, axis=1, keepdims=True), jnp.max(fresh, axis=1, keepdims=True)
    )
    weights = jnp.exp(scores - peak)
    fresh_weights = jnp.exp(fresh - peak)
    total = jnp.sum(weights, axis=1, keepdims=True) + jnp.sum(fresh_weights, axis=1, keepdims=True)
    mixed = dot(weights.astype(BF16), values) + dot(fresh_weights.astype(BF16), fresh_values)
    mixed = mixed / total
    return jnp.concatenate([mixed[h * steps : (h + 1) * steps] for h in range(heads)], axis=1)


def kernel(
    lengths_hbm, finished_hbm, mig_hbm, query_hbm, new_keys_hbm, new_values_hbm,
    keys_hbm, values_hbm, weight_hbm,
    out,
    lengths, finished, mig, query, new_keys, new_values, keys, values, weight,
    ask, asked, relay, part, reduced, moved_part, moved_in, total, chunk, gathered,
    load_sem, ask_send, ask_recv, relay_send, relay_recv,
    rs_send, rs_recv, mv_send, mv_recv, ag_send, ag_recv, ready, open_sem,
    *, slots, steps, heads, n_dp, n_t, parity,
):
    g, t = lax.axis_index("dp"), lax.axis_index("tensor")
    up, down = lax.rem(g + 1, n_dp), lax.rem(g + n_dp - 1, n_dp)
    rows = slots * steps
    is_src = lax.rem(g, 2) == parity
    is_dst = jnp.logical_not(is_src)
    late_dst = jnp.logical_and(lax.rem(g, 16) == 0, is_dst)
    late_src = jnp.logical_and(lax.rem(g, 16) == 15, is_src)
    relays = jnp.logical_and(jnp.logical_and(lax.rem(g, 16) == 7, is_src), t == 0)
    relay_group = lax.rem(g + n_dp - 9, n_dp)
    relay_dst = lax.rem(g + 9, n_dp)
    relay_src = lax.rem(g + 8, n_dp)
    late = parity == 1

    loads = [
        pltpu.make_async_copy(src, dst, load_sem.at[i])
        for i, (src, dst) in enumerate(
            [
                (mig_hbm, mig), (query_hbm, query), (new_keys_hbm, new_keys),
                (new_values_hbm, new_values), (lengths_hbm, lengths),
                (finished_hbm, finished), (keys_hbm, keys), (values_hbm, values),
                (weight_hbm, weight),
            ]
        )
    ]
    for load in loads:
        load.start()

    barrier = pltpu.get_barrier_semaphore()

    def greet(group, other):
        pl.semaphore_signal(barrier, inc=1, device_id=(group, other), device_id_type=MESH)

    for j in range(n_t):

        @pl.when(t != j)
        def _():
            greet(g, j)

    if late:

        @pl.when(jnp.logical_and(is_src, jnp.logical_not(late_src)))
        def _():
            for j in range(n_t):
                greet(up, j)

        @pl.when(late_dst)
        def _():
            for j in range(n_t):
                greet(down, j)

        @pl.when(relays)
        def _():
            for j in range(n_t):
                greet(relay_dst, j)
                greet(relay_src, j)

    else:

        @pl.when(is_src)
        def _():
            for j in range(n_t):
                greet(up, j)

    for load in loads[:6]:
        load.wait()
    sending = mig[0:1, :] == g
    arriving = mig[1:2, :] == g
    has_send = jnp.sum(sending.astype(jnp.int32)) > 0
    has_arrival = jnp.sum(arriving.astype(jnp.int32)) > 0
    sent_row = jnp.sum(jnp.where(sending, mig[2:3, :], 0))
    arrival_slot = jnp.sum(jnp.where(arriving, mig[3:4, :], 0))

    def flat(ref):
        return jnp.concatenate([ref[s].astype(F32) for s in range(steps)], axis=0)

    i, j = grid_ids((rows + steps, rows))
    slot = jnp.where(i < rows, i // steps, arrival_slot)
    order = one_hot(j == lax.rem(i, steps) * slots + slot)
    by_slot = dot(order, flat(query).astype(BF16))
    fresh = jnp.concatenate([flat(new_keys), flat(new_values)], axis=1).astype(BF16)
    fresh_by_slot = dot(order, fresh)
    ask[0 : heads * steps, :] = stack_heads(by_slot[rows:], heads).astype(BF16)
    ask[heads * steps :, :] = stack_heads(fresh_by_slot[rows:], 2).astype(BF16)

    zeros = jnp.zeros((16 - steps, HD), F32)

    def pad(x):
        return jnp.concatenate([x, zeros], axis=0).astype(BF16)

    loads[6].wait()
    loads[7].wait()
    attended = []
    for r in range(slots):
        mine = slice(r * steps, (r + 1) * steps)
        mixed = attend(
            stack_heads(by_slot[mine], heads).astype(BF16),
            keys[r], values[r],
            pad(fresh_by_slot[mine, :HD]), pad(fresh_by_slot[mine, HD:]),
            lengths[r] * BLOCK, steps, heads,
        )
        stays = jnp.logical_and(
            finished[r] == 0, jnp.logical_not(jnp.logical_and(has_send, sent_row == r))
        )
        attended.append(jnp.where(stays, mixed, 0.0))
    attended = jnp.concatenate(attended, axis=0).astype(BF16)
    i, j = grid_ids((rows, rows))
    to_steps = one_hot(j == lax.rem(i, slots) * steps + i // slots)
    attended = dot(to_steps, attended).astype(BF16)

    loads[8].wait()
    half = rows // 2
    for c in range(10):
        block = dot(attended, weight[:, 256 * c : 256 * (c + 1)]).astype(BF16)
        for k in range(2):
            for h in range(2):
                piece = block[h * half : (h + 1) * half, k * LANES : (k + 1) * LANES]
                if c < 8:
                    part[c, 2 * k + h] = piece
                else:
                    part[2 * (2 * (c - 8) + k) + h, 4] = piece

    if late:
        greeted = (n_t - 1) + jnp.where(
            is_src, jnp.where(late_src, n_t + 1, 0), jnp.where(late_dst, 1, n_t)
        )
    else:
        greeted = (n_t - 1) + jnp.where(is_src, 0, n_t)
    pl.semaphore_wait(barrier, greeted)

    def ask_copy(group, other):
        return pltpu.make_async_remote_copy(
            ask, asked, ask_send, ask_recv, device_id=(group, other), device_id_type=MESH
        )

    def relay_copy(slot, group):
        return pltpu.make_async_remote_copy(
            ask, relay.at[slot], ask_send, relay_recv.at[slot],
            device_id=(group, 0), device_id_type=MESH,
        )

    def pass_copy(j):
        return pltpu.make_async_remote_copy(
            relay.at[j], asked, relay_send.at[j], ask_recv,
            device_id=(relay_src, j), device_id_type=MESH,
        )

    def rs_copy(j, slot):
        return pltpu.make_async_remote_copy(
            part.at[j], reduced.at[slot], rs_send.at[j], rs_recv.at[slot],
            device_id=(g, j), device_id_type=MESH,
        )

    def mv_copy(j, slot):
        return pltpu.make_async_remote_copy(
            moved_part.at[j], moved_in.at[slot], mv_send.at[j], mv_recv.at[slot],
            device_id=(up, j), device_id_type=MESH,
        )

    def ag_copy(j, slot):
        return pltpu.make_async_remote_copy(
            chunk, gathered.at[slot], ag_send.at[j], ag_recv.at[slot],
            device_id=(g, j), device_id_type=MESH,
        )

    def tell(sem, group, j):
        pl.semaphore_signal(sem, inc=1, device_id=(group, j), device_id_type=MESH)

    if late:

        @pl.when(late_dst)
        def _():
            relay_copy(t, relay_group).start()

        @pl.when(late_src)
        def _():
            tell(open_sem, lax.rem(g + n_dp - 8, n_dp), 0)

        @pl.when(jnp.logical_and(is_dst, jnp.logical_not(late_dst)))
        def _():
            ask_copy(down, t).start()
            for j in range(n_t):
                tell(ready, down, j)

    else:

        @pl.when(is_dst)
        def _():
            ask_copy(down, t).start()
            for j in range(n_t):
                tell(ready, down, j)

    for j in reversed(range(n_t)):

        @pl.when(t != j)
        def _():
            rs_copy(j, t).start()

    if late:

        @pl.when(relays)
        def _():
            pl.semaphore_wait(open_sem, n_t)
            for j in reversed(range(n_t)):
                relay_copy(j, g).wait_recv()
                pass_copy(j).start()

    @pl.when(is_src)
    def _():
        ask_copy(g, t).wait_recv()
        asked_fresh = asked[heads * steps :, :].astype(F32)
        moved = attend(
            asked[0 : heads * steps, :],
            keys[sent_row], values[sent_row],
            pad(asked_fresh[:steps]), pad(asked_fresh[steps:]),
            lengths[sent_row] * BLOCK, steps, heads,
        )
        moved = jnp.where(has_send, moved, 0.0).astype(BF16)
        for c in range(10):
            block = dot(moved, weight[:, 256 * c : 256 * (c + 1)])
            piece = jnp.concatenate([block[:, :LANES], block[:, LANES:]], axis=0).astype(BF16)
            if c < 8:
                moved_part[c, 0] = piece
            else:
                for j in range(4):
                    moved_part[4 * (c - 8) + j, 1] = piece
        if late:

            @pl.when(jnp.logical_not(late_src))
            def _():
                pl.semaphore_wait(ready, n_t)

        else:
            pl.semaphore_wait(ready, n_t)
        for j in reversed(range(n_t)):
            mv_copy(j, t).start()

    reduced[t] = part[t]
    for j in range(n_t):

        @pl.when(t != j)
        def _():
            rs_copy(j, j).wait_recv()

    acc = reduced[0].astype(F32)
    for j in range(1, n_t):
        acc = acc + reduced[j].astype(F32)
    total[...] = acc

    @pl.when(is_dst)
    def _():
        for j in range(n_t):
            mv_copy(j, j).wait_recv()
        arrived = moved_in[0].astype(F32)
        for j in range(1, n_t):
            arrived = arrived + moved_in[j].astype(F32)
        arrived = jnp.where(has_arrival, arrived, 0.0).astype(BF16)
        i, j = grid_ids((rows, steps))
        place = one_hot(jnp.logical_and(lax.rem(i, slots) == arrival_slot, i // slots == j))
        lo = dot(place, arrived[0, :steps])
        hi = dot(place, arrived[0, steps:])
        extra = dot(
            place, jnp.where(lax.rem(t // 2, 2) == 0, arrived[1, :steps], arrived[1, steps:])
        )
        extra = jnp.where(lax.rem(t, 2) == 0, extra[:half], extra[half:])
        total[0] += lo[:half]
        total[1] += lo[half:]
        total[2] += hi[:half]
        total[3] += hi[half:]
        total[4] += extra

    chunk[...] = total[...].astype(BF16)
    for j in range(n_t):

        @pl.when(t != j)
        def _():
            ag_copy(j, t).start()

    gathered[t] = chunk[...]
    for j in range(n_t):

        @pl.when(t != j)
        def _():
            ag_copy(j, j).wait_recv()

    for j in range(n_t):
        for k in range(2):
            for h in range(2):
                out[h * half : (h + 1) * half, (2 * j + k) * LANES : (2 * j + k + 1) * LANES] = (
                    gathered[j, 2 * k + h]
                )
        tile = 2 * n_t + j // 2
        h = j % 2
        out[h * half : (h + 1) * half, tile * LANES : (tile + 1) * LANES] = gathered[j, 4]

    for j in range(n_t):

        @pl.when(t != j)
        def _():
            rs_copy(j, t).wait_send()
            ag_copy(j, t).wait_send()

    @pl.when(is_src)
    def _():
        for j in range(n_t):
            mv_copy(j, t).wait_send()

    @pl.when(is_dst)
    def _():
        ask_copy(down, t).wait_send()

    if late:

        @pl.when(relays)
        def _():
            for j in range(n_t):
                pass_copy(j).wait_send()


def parity_kernel(mig_hbm, out, mig, sem):
    load = pltpu.make_async_copy(mig_hbm, mig, sem)
    load.start()
    load.wait()
    out[0] = lax.rem(mig[0, 0], 2)


def source_parity(moves):
    return pl.pallas_call(
        parity_kernel,
        out_shape=jax.ShapeDtypeStruct((1,), jnp.int32),
        in_specs=[pl.BlockSpec(memory_space=pltpu.HBM)],
        out_specs=pl.BlockSpec(memory_space=pltpu.SMEM),
        scratch_shapes=[pltpu.SMEM(moves.shape, jnp.int32), pltpu.SemaphoreType.DMA],
    )(moves)[0]


def project(parity, n_dp, n_t, *operands):
    lengths, finished, moves, queries, new_keys, new_values, keys, values, weight = operands
    steps, slots, width = queries.shape
    features = weight.shape[1]
    heads = width // HD
    rows = steps * slots
    dma = pltpu.SemaphoreType.DMA
    regular = pltpu.SemaphoreType.REGULAR
    asks = ((heads + 2) * steps, HD)
    pieces = (n_t, 5, rows // 2, LANES)
    moved = (n_t, 2, 2 * steps, LANES)
    return pl.pallas_call(
        functools.partial(
            kernel, slots=slots, steps=steps, heads=heads, n_dp=n_dp, n_t=n_t, parity=parity
        ),
        out_shape=jax.ShapeDtypeStruct((rows, features), BF16),
        in_specs=[pl.BlockSpec(memory_space=pltpu.HBM)] * 9,
        out_specs=pl.BlockSpec(memory_space=pltpu.VMEM),
        scratch_shapes=[
            pltpu.SMEM(lengths.shape, jnp.int32),
            pltpu.SMEM(finished.shape, jnp.int32),
            pltpu.VMEM(moves.shape, jnp.int32),
            pltpu.VMEM(queries.shape, BF16),
            pltpu.VMEM(new_keys.shape, BF16),
            pltpu.VMEM(new_values.shape, BF16),
            pltpu.VMEM(keys.shape, BF16),
            pltpu.VMEM(values.shape, BF16),
            pltpu.VMEM(weight.shape, BF16),
            pltpu.VMEM(asks, BF16),
            pltpu.VMEM(asks, BF16),
            pltpu.VMEM((n_t,) + asks, BF16),
            pltpu.VMEM(pieces, BF16),
            pltpu.VMEM(pieces, BF16),
            pltpu.VMEM(moved, BF16),
            pltpu.VMEM(moved, BF16),
            pltpu.VMEM(pieces[1:], F32),
            pltpu.VMEM(pieces[1:], BF16),
            pltpu.VMEM(pieces, BF16),
            dma((9,)), dma, dma, dma((n_t,)), dma((n_t,)),
            dma((n_t,)), dma((n_t,)), dma((n_t,)), dma((n_t,)), dma((n_t,)), dma((n_t,)),
            regular, regular,
        ],
        compiler_params=pltpu.CompilerParams(
            collective_id=parity, has_side_effects=True, vmem_limit_bytes=48 << 20
        ),
    )(*operands)


def per_device(n_dp, n_t, cache_keys, cache_values, lengths, finished, migrations, queries,
               new_keys, new_values, out_weight):
    steps, slots, _ = queries.shape
    moves = migrations.T
    result = lax.cond(
        source_parity(moves) == 0,
        functools.partial(project, 0, n_dp, n_t),
        functools.partial(project, 1, n_dp, n_t),
        lengths, finished, moves, queries, new_keys, new_values,
        cache_keys, cache_values, out_weight,
    )
    return result.reshape(steps, slots, out_weight.shape[1])


def solution(mesh):
    sizes = dict(zip(mesh.axis_names, mesh.devices.shape))
    return jax.shard_map(
        functools.partial(per_device, sizes["dp"], sizes["tensor"]),
        mesh=mesh,
        in_specs=(
            P("dp", None, "tensor"),
            P("dp", None, "tensor"),
            P("dp"),
            P("dp"),
            P(),
            P(None, "dp", "tensor"),
            P(None, "dp", "tensor"),
            P(None, "dp", "tensor"),
            P("tensor", None),
        ),
        out_specs=P(None, "dp", None),
        check_vma=False,
    )
```

```python
import functools

import jax
import jax.numpy as jnp
from jax import lax
from jax.experimental import pallas as pl
from jax.experimental.pallas import tpu as pltpu
from jax.sharding import PartitionSpec as P

HD = 128
BLOCK = 512
LANES = 128
MESH = pl.DeviceIdType.MESH
F32 = jnp.float32
BF16 = jnp.bfloat16


def one_hot(mask):
    return jnp.where(mask, 1.0, 0.0).astype(BF16)


def grid_ids(shape):
    return (
        lax.broadcasted_iota(jnp.int32, shape, 0),
        lax.broadcasted_iota(jnp.int32, shape, 1),
    )


def dot(a, b):
    return lax.dot_general(a, b, (((1,), (0,)), ((), ())), preferred_element_type=F32)


def dot_t(a, b):
    return lax.dot_general(a, b, (((1,), (1,)), ((), ())), preferred_element_type=F32)


def stack_heads(rows, heads):
    return jnp.concatenate([rows[:, h * HD : (h + 1) * HD] for h in range(heads)], axis=0)


def attend(query, keys, values, fresh_keys, fresh_values, limit, steps, heads):
    scale = 1.0 / HD**0.5
    scores = dot_t(query, keys) * scale
    fresh = dot_t(query, fresh_keys) * scale
    _, position = grid_ids(scores.shape)
    scores = jnp.where(position < limit, scores, -1e30)
    row, token = grid_ids(fresh.shape)
    fresh = jnp.where(token <= lax.rem(row, steps), fresh, -1e30)
    peak = jnp.maximum(
        jnp.max(scores, axis=1, keepdims=True), jnp.max(fresh, axis=1, keepdims=True)
    )
    weights = jnp.exp(scores - peak)
    fresh_weights = jnp.exp(fresh - peak)
    total = jnp.sum(weights, axis=1, keepdims=True) + jnp.sum(fresh_weights, axis=1, keepdims=True)
    mixed = dot(weights.astype(BF16), values) + dot(fresh_weights.astype(BF16), fresh_values)
    mixed = mixed / total
    return jnp.concatenate([mixed[h * steps : (h + 1) * steps] for h in range(heads)], axis=1)


def kernel(
    lengths_hbm, finished_hbm, mig_hbm, query_hbm, new_keys_hbm, new_values_hbm,
    keys_hbm, values_hbm, weight_hbm,
    out,
    lengths, finished, mig, query, new_keys, new_values, keys, values, weight,
    ask, asked, relay, part, reduced, moved_part, moved_in, total, chunk, gathered,
    load_sem, ask_send, ask_recv, relay_send, relay_recv,
    rs_send, rs_recv, mv_send, mv_recv, ag_send, ag_recv, here, ready, open_sem,
    *, slots, steps, heads, n_dp, n_t, parity,
):
    g, t = lax.axis_index("dp"), lax.axis_index("tensor")
    up, down = lax.rem(g + 1, n_dp), lax.rem(g + n_dp - 1, n_dp)
    rows = slots * steps
    is_src = lax.rem(g, 2) == parity
    is_dst = jnp.logical_not(is_src)
    far = parity == 1
    place16 = lax.rem(g, 16)
    far_src_first = jnp.logical_and(is_src, place16 == 7)
    far_dst_last = jnp.logical_and(is_dst, place16 == 8)
    far_src_last = jnp.logical_and(is_src, place16 == 15)
    far_dst_first = jnp.logical_and(is_dst, place16 == 0)
    near = jnp.logical_or(
        jnp.logical_and(is_src, jnp.logical_and(place16 != 7, place16 != 15)),
        jnp.logical_and(is_dst, jnp.logical_and(place16 != 8, place16 != 0)),
    )
    relays = jnp.logical_and(far_src_first, t == 0)
    relay_of_dst = lax.rem(g + n_dp - 9, n_dp)
    relay_of_src = lax.rem(g + n_dp - 8, n_dp)
    relay_dst = lax.rem(g + 9, n_dp)
    relay_src = lax.rem(g + 8, n_dp)

    def when(*conditions):
        return pl.when(functools.reduce(jnp.logical_and, conditions))

    pairs = [
        (mig_hbm, mig), (query_hbm, query), (new_keys_hbm, new_keys),
        (new_values_hbm, new_values), (lengths_hbm, lengths), (finished_hbm, finished),
    ]
    pairs += [(keys_hbm.at[r], keys.at[r]) for r in range(slots)]
    pairs += [(values_hbm.at[r], values.at[r]) for r in range(slots)]
    pairs += [
        (weight_hbm.at[:, pl.ds(256 * c, 256)], weight.at[:, pl.ds(256 * c, 256)])
        for c in range(10)
    ]
    loads = [
        pltpu.make_async_copy(src, dst, load_sem.at[i]) for i, (src, dst) in enumerate(pairs)
    ]
    for load in loads:
        load.start()
    key_loads, value_loads = loads[6 : 6 + slots], loads[6 + slots : 6 + 2 * slots]
    weight_loads = loads[6 + 2 * slots :]

    barrier = pltpu.get_barrier_semaphore()

    def greet(group, other):
        pl.semaphore_signal(barrier, inc=1, device_id=(group, other), device_id_type=MESH)

    def tell(sem, group, other):
        pl.semaphore_signal(sem, inc=1, device_id=(group, other), device_id_type=MESH)

    near_src = jnp.logical_and(is_src, near) if far else is_src
    near_dst = jnp.logical_and(is_dst, near) if far else is_dst

    def rank_of(group, other):
        return jnp.where(jnp.logical_and(group == 0, other == 0), n_t, other)

    rank = rank_of(g, t)
    last = rank == n_t
    before_last = jnp.logical_and(g == 0, t > 0)

    for j in range(n_t):

        @when(rank_of(g, j) > rank)
        def _():
            greet(g, j)

        @when(near_src, j >= rank)
        def _():
            greet(up, j)

        @when(near_dst, rank_of(down, j) >= t)
        def _():
            greet(down, j)

    if far:

        @when(far_src_first)
        def _():
            for j in range(n_t):
                greet(up, j)

        @when(far_dst_first, jnp.logical_not(last))
        def _():
            for j in range(n_t):
                greet(down, j)

        @when(relays)
        def _():
            for j in range(n_t):
                greet(relay_dst, j)
                greet(relay_src, j)

        greeted = jnp.where(
            near, t + 1,
            jnp.where(
                far_dst_last, n_t,
                jnp.where(far_src_last, n_t + 1, jnp.where(far_dst_first, 1, 0)),
            ),
        )
        greeted = jnp.where(last, n_t, t + greeted)
        fewer = jnp.logical_or(before_last, g == n_dp - 1)
    else:
        greeted = jnp.where(last, 2 * n_t - 1, 2 * t + 1)
        fewer = jnp.logical_or(before_last, g == 1)
    greeted = greeted - jnp.where(fewer, 1, 0)

    @when(greeted > 0)
    def _():
        pl.semaphore_wait(barrier, greeted)


    for j in range(n_t):

        @when(rank_of(g, j) < rank)
        def _():
            tell(here.at[t], g, j)

        @when(near_dst, rank_of(down, j) < t)
        def _():
            tell(ready.at[t], down, j)

    ask_later = jnp.logical_and(g == 1, t == 0)
    if far:

        @when(far_dst_last)
        def _():
            for j in range(n_t):
                tell(ready.at[t], down, j)

        @when(far_src_last)
        def _():
            tell(open_sem.at[t], relay_of_src, 0)

    else:

        @when(last)
        def _():
            tell(ready.at[0], up, 0)

    def ask_copy(group, other):
        return pltpu.make_async_remote_copy(
            ask, asked, ask_send, ask_recv, device_id=(group, other), device_id_type=MESH
        )

    def relay_copy(slot, group):
        return pltpu.make_async_remote_copy(
            ask, relay.at[slot], ask_send, relay_recv.at[slot],
            device_id=(group, 0), device_id_type=MESH,
        )

    def pass_copy(j):
        return pltpu.make_async_remote_copy(
            relay.at[j], asked, relay_send.at[j], ask_recv,
            device_id=(relay_src, j), device_id_type=MESH,
        )

    def rs_copy(j, slot):
        return pltpu.make_async_remote_copy(
            part.at[j], reduced.at[slot], rs_send.at[j], rs_recv.at[slot],
            device_id=(g, j), device_id_type=MESH,
        )

    def mv_copy(j, slot):
        return pltpu.make_async_remote_copy(
            moved_part.at[j], moved_in.at[slot], mv_send.at[j], mv_recv.at[slot],
            device_id=(up, j), device_id_type=MESH,
        )

    def ag_copy(j, slot):
        return pltpu.make_async_remote_copy(
            chunk, gathered.at[slot], ag_send.at[j], ag_recv.at[slot],
            device_id=(g, j), device_id_type=MESH,
        )

    for load in loads[:6]:
        load.wait()
    sending = mig[0:1, :] == g
    arriving = mig[1:2, :] == g
    has_send = jnp.sum(sending.astype(jnp.int32)) > 0
    has_arrival = jnp.sum(arriving.astype(jnp.int32)) > 0
    sent_row = jnp.sum(jnp.where(sending, mig[2:3, :], 0))
    arrival_slot = jnp.sum(jnp.where(arriving, mig[3:4, :], 0))

    def flat(ref):
        return jnp.concatenate([ref[s].astype(F32) for s in range(steps)], axis=0)

    i, j = grid_ids((rows + steps, rows))
    slot = jnp.where(i < rows, i // steps, arrival_slot)
    order = one_hot(j == lax.rem(i, steps) * slots + slot)
    by_slot = dot(order, flat(query).astype(BF16))
    fresh = jnp.concatenate([flat(new_keys), flat(new_values)], axis=1).astype(BF16)
    fresh_by_slot = dot(order, fresh)
    ask[0 : heads * steps, :] = stack_heads(by_slot[rows:], heads).astype(BF16)
    ask[heads * steps :, :] = stack_heads(fresh_by_slot[rows:], 2).astype(BF16)

    if far:

        @when(is_dst, jnp.logical_not(far_dst_first))
        def _():
            ask_copy(down, t).start()

        @when(far_dst_first)
        def _():
            relay_copy(t, relay_of_dst).start()

    else:

        @when(is_dst, jnp.logical_not(ask_later))
        def _():
            ask_copy(down, t).start()

    zeros = jnp.zeros((16 - steps, HD), F32)

    def pad(x):
        return jnp.concatenate([x, zeros], axis=0).astype(BF16)

    attended = []
    for r in range(slots):
        key_loads[r].wait()
        value_loads[r].wait()
        mine = slice(r * steps, (r + 1) * steps)
        mixed = attend(
            stack_heads(by_slot[mine], heads).astype(BF16),
            keys[r], values[r],
            pad(fresh_by_slot[mine, :HD]), pad(fresh_by_slot[mine, HD:]),
            lengths[r] * BLOCK, steps, heads,
        )
        stays = jnp.logical_and(
            finished[r] == 0, jnp.logical_not(jnp.logical_and(has_send, sent_row == r))
        )
        attended.append(jnp.where(stays, mixed, 0.0))
    attended = jnp.concatenate(attended, axis=0).astype(BF16)
    i, j = grid_ids((rows, rows))
    to_steps = one_hot(j == lax.rem(i, slots) * steps + i // slots)
    attended = dot(to_steps, attended).astype(BF16)

    half = rows // 2

    def put_part(c, block):
        block = block.astype(BF16)
        for k in range(2):
            for h in range(2):
                piece = block[h * half : (h + 1) * half, k * LANES : (k + 1) * LANES]
                if c < 8:
                    part[c, 2 * k + h] = piece
                else:
                    part[2 * (2 * (c - 8) + k) + h, 4] = piece

    def put_moved(c, block):
        piece = jnp.concatenate([block[:, :LANES], block[:, LANES:]], axis=0).astype(BF16)
        if c < 8:
            moved_part[c, 0] = piece
        else:
            for j in range(4):
                moved_part[4 * (c - 8) + j, 1] = piece

    def columns(c):
        return weight[:, 256 * c : 256 * (c + 1)]

    def attend_moved():
        ask_copy(g, t).wait_recv()
        asked_fresh = asked[heads * steps :, :].astype(F32)
        moved = attend(
            asked[0 : heads * steps, :],
            keys[sent_row], values[sent_row],
            pad(asked_fresh[:steps]), pad(asked_fresh[steps:]),
            lengths[sent_row] * BLOCK, steps, heads,
        )
        return jnp.where(has_send, moved, 0.0).astype(BF16)

    def send_all(parts, moved):
        for j in reversed(range(n_t)):
            if moved:

                @when(near_src, j <= rank)
                def _():
                    mv_copy(j, t).start()

            if parts:

                @when(rank_of(g, j) < rank)
                def _():
                    rs_copy(j, t).start()

        for j in list(range(1, n_t)) + [0]:
            if moved:

                @when(near_src, j > rank)
                def _():
                    pl.semaphore_wait(ready.at[j], 1)
                    mv_copy(j, t).start()

            if parts:

                @when(rank_of(g, j) > rank)
                def _():
                    pl.semaphore_wait(here.at[j], 1)
                    rs_copy(j, t).start()

        if moved and far:

            @when(far_src_first)
            def _():
                for j in range(n_t):
                    pl.semaphore_wait(ready.at[j], 1)
                    mv_copy(j, t).start()

            @when(far_src_last)
            def _():
                for j in range(n_t):
                    mv_copy(j, t).start()

    if far:
        for c in range(10):
            weight_loads[c].wait()
            put_part(c, dot(attended, columns(c)))
        send_all(True, False)

        @when(relays)
        def _():
            for j in range(n_t):
                pl.semaphore_wait(open_sem.at[j], 1)
                relay_copy(j, g).wait_recv()
                pass_copy(j).start()

        @when(is_src)
        def _():
            moved = attend_moved()
            for c in range(10):
                put_moved(c, dot(moved, columns(c)))
            send_all(False, True)

    else:

        @when(is_src)
        def _():
            both = jnp.concatenate([attended.astype(F32), attend_moved().astype(F32)], axis=0)
            both = both.astype(BF16)
            for c in range(10):
                weight_loads[c].wait()
                block = dot(both, columns(c))
                put_part(c, block[:rows])
                put_moved(c, block[rows:])
            send_all(True, True)

        @when(ask_later)
        def _():
            pl.semaphore_wait(ready.at[0], 1)
            ask_copy(down, t).start()

        @when(is_dst)
        def _():
            for c in range(10):
                weight_loads[c].wait()
                put_part(c, dot(attended, columns(c)))
            send_all(True, False)

    reduced[t] = part[t]
    for j in range(n_t):

        @pl.when(t != j)
        def _():
            rs_copy(j, j).wait_recv()

    acc = reduced[0].astype(F32)
    for j in range(1, n_t):
        acc = acc + reduced[j].astype(F32)
    total[...] = acc

    @pl.when(is_dst)
    def _():
        for j in range(n_t):
            mv_copy(j, j).wait_recv()
        arrived = moved_in[0].astype(F32)
        for j in range(1, n_t):
            arrived = arrived + moved_in[j].astype(F32)
        arrived = jnp.where(has_arrival, arrived, 0.0).astype(BF16)
        i, j = grid_ids((rows, steps))
        place = one_hot(jnp.logical_and(lax.rem(i, slots) == arrival_slot, i // slots == j))
        lo = dot(place, arrived[0, :steps])
        hi = dot(place, arrived[0, steps:])
        extra = dot(
            place, jnp.where(lax.rem(t // 2, 2) == 0, arrived[1, :steps], arrived[1, steps:])
        )
        extra = jnp.where(lax.rem(t, 2) == 0, extra[:half], extra[half:])
        total[0] += lo[:half]
        total[1] += lo[half:]
        total[2] += hi[:half]
        total[3] += hi[half:]
        total[4] += extra

    chunk[...] = total[...].astype(BF16)
    for j in range(n_t):

        @pl.when(t != j)
        def _():
            ag_copy(j, t).start()

    gathered[t] = chunk[...]
    for j in range(n_t):

        @pl.when(t != j)
        def _():
            ag_copy(j, j).wait_recv()

    for j in range(n_t):
        for k in range(2):
            for h in range(2):
                out[h * half : (h + 1) * half, (2 * j + k) * LANES : (2 * j + k + 1) * LANES] = (
                    gathered[j, 2 * k + h]
                )
        tile = 2 * n_t + j // 2
        h = j % 2
        out[h * half : (h + 1) * half, tile * LANES : (tile + 1) * LANES] = gathered[j, 4]

    for j in range(n_t):

        @pl.when(t != j)
        def _():
            rs_copy(j, t).wait_send()
            ag_copy(j, t).wait_send()

    @pl.when(is_src)
    def _():
        for j in range(n_t):
            mv_copy(j, t).wait_send()

    @pl.when(is_dst)
    def _():
        ask_copy(down, t).wait_send()

    if far:

        @pl.when(relays)
        def _():
            for j in range(n_t):
                pass_copy(j).wait_send()


def parity_kernel(mig_hbm, out, mig, sem):
    load = pltpu.make_async_copy(mig_hbm, mig, sem)
    load.start()
    load.wait()
    out[0] = lax.rem(mig[0, 0], 2)


def source_parity(moves):
    return pl.pallas_call(
        parity_kernel,
        out_shape=jax.ShapeDtypeStruct((1,), jnp.int32),
        in_specs=[pl.BlockSpec(memory_space=pltpu.HBM)],
        out_specs=pl.BlockSpec(memory_space=pltpu.SMEM),
        scratch_shapes=[pltpu.SMEM(moves.shape, jnp.int32), pltpu.SemaphoreType.DMA],
    )(moves)[0]


def project(parity, n_dp, n_t, *operands):
    lengths, finished, moves, queries, new_keys, new_values, keys, values, weight = operands
    steps, slots, width = queries.shape
    features = weight.shape[1]
    heads = width // HD
    rows = steps * slots
    dma = pltpu.SemaphoreType.DMA
    regular = pltpu.SemaphoreType.REGULAR
    asks = ((heads + 2) * steps, HD)
    pieces = (n_t, 5, rows // 2, LANES)
    moved = (n_t, 2, 2 * steps, LANES)
    return pl.pallas_call(
        functools.partial(
            kernel, slots=slots, steps=steps, heads=heads, n_dp=n_dp, n_t=n_t, parity=parity
        ),
        out_shape=jax.ShapeDtypeStruct((rows, features), BF16),
        in_specs=[pl.BlockSpec(memory_space=pltpu.HBM)] * 9,
        out_specs=pl.BlockSpec(memory_space=pltpu.VMEM),
        scratch_shapes=[
            pltpu.SMEM(lengths.shape, jnp.int32),
            pltpu.SMEM(finished.shape, jnp.int32),
            pltpu.VMEM(moves.shape, jnp.int32),
            pltpu.VMEM(queries.shape, BF16),
            pltpu.VMEM(new_keys.shape, BF16),
            pltpu.VMEM(new_values.shape, BF16),
            pltpu.VMEM(keys.shape, BF16),
            pltpu.VMEM(values.shape, BF16),
            pltpu.VMEM(weight.shape, BF16),
            pltpu.VMEM(asks, BF16),
            pltpu.VMEM(asks, BF16),
            pltpu.VMEM((n_t,) + asks, BF16),
            pltpu.VMEM(pieces, BF16),
            pltpu.VMEM(pieces, BF16),
            pltpu.VMEM(moved, BF16),
            pltpu.VMEM(moved, BF16),
            pltpu.VMEM(pieces[1:], F32),
            pltpu.VMEM(pieces[1:], BF16),
            pltpu.VMEM(pieces, BF16),
            dma((6 + 2 * slots + 10,)), dma, dma, dma((n_t,)), dma((n_t,)),
            dma((n_t,)), dma((n_t,)), dma((n_t,)), dma((n_t,)), dma((n_t,)), dma((n_t,)),
            regular((n_t,)), regular((n_t,)), regular((n_t,)),
        ],
        compiler_params=pltpu.CompilerParams(
            collective_id=parity, has_side_effects=True, vmem_limit_bytes=48 << 20
        ),
    )(*operands)


def per_device(n_dp, n_t, cache_keys, cache_values, lengths, finished, migrations, queries,
               new_keys, new_values, out_weight):
    steps, slots, _ = queries.shape
    moves = migrations.T
    result = lax.cond(
        source_parity(moves) == 0,
        functools.partial(project, 0, n_dp, n_t),
        functools.partial(project, 1, n_dp, n_t),
        lengths, finished, moves, queries, new_keys, new_values,
        cache_keys, cache_values, out_weight,
    )
    return result.reshape(steps, slots, out_weight.shape[1])


def solution(mesh):
    sizes = dict(zip(mesh.axis_names, mesh.devices.shape))
    return jax.shard_map(
        functools.partial(per_device, sizes["dp"], sizes["tensor"]),
        mesh=mesh,
        in_specs=(
            P("dp", None, "tensor"),
            P("dp", None, "tensor"),
            P("dp"),
            P("dp"),
            P(),
            P(None, "dp", "tensor"),
            P(None, "dp", "tensor"),
            P(None, "dp", "tensor"),
            P("tensor", None),
        ),
        out_specs=P(None, "dp", None),
        check_vma=False,
    )
```

```python
import functools

import jax
import jax.numpy as jnp
from jax import lax
from jax.experimental import pallas as pl
from jax.experimental.pallas import tpu as pltpu
from jax.sharding import PartitionSpec as P

HD = 128
BLOCK = 512
LANES = 128
HELPER = 3
MESH = pl.DeviceIdType.MESH
F32 = jnp.float32
BF16 = jnp.bfloat16


def one_hot(mask):
    return jnp.where(mask, 1.0, 0.0).astype(BF16)


def grid_ids(shape):
    return (
        lax.broadcasted_iota(jnp.int32, shape, 0),
        lax.broadcasted_iota(jnp.int32, shape, 1),
    )


def dot(a, b):
    return lax.dot_general(a, b, (((1,), (0,)), ((), ())), preferred_element_type=F32)


def dot_t(a, b):
    return lax.dot_general(a, b, (((1,), (1,)), ((), ())), preferred_element_type=F32)


def stack_heads(rows, heads):
    return jnp.concatenate([rows[:, h * HD : (h + 1) * HD] for h in range(heads)], axis=0)


def attend(query, keys, values, fresh_keys, fresh_values, limit, steps, heads):
    scale = 1.0 / HD**0.5
    scores = dot_t(query, keys) * scale
    fresh = dot_t(query, fresh_keys) * scale
    _, position = grid_ids(scores.shape)
    scores = jnp.where(position < limit, scores, -1e30)
    row, token = grid_ids(fresh.shape)
    fresh = jnp.where(token <= lax.rem(row, steps), fresh, -1e30)
    peak = jnp.maximum(
        jnp.max(scores, axis=1, keepdims=True), jnp.max(fresh, axis=1, keepdims=True)
    )
    weights = jnp.exp(scores - peak)
    fresh_weights = jnp.exp(fresh - peak)
    total = jnp.sum(weights, axis=1, keepdims=True) + jnp.sum(fresh_weights, axis=1, keepdims=True)
    mixed = dot(weights.astype(BF16), values) + dot(fresh_weights.astype(BF16), fresh_values)
    mixed = mixed / total
    return jnp.concatenate([mixed[h * steps : (h + 1) * steps] for h in range(heads)], axis=1)


def kernel(
    lengths_hbm, finished_hbm, mig_hbm, query_hbm, new_keys_hbm, new_values_hbm,
    keys_hbm, values_hbm, weight_hbm,
    out,
    lengths, finished, mig, query, new_keys, new_values, keys, values, weight,
    ask, asked, relay, part, reduced, moved_part, moved_in, far_part, far_in, far_row, total, chunk,
    gathered,
    load_sem, ask_send, ask_recv, relay_send, relay_recv,
    rs_send, rs_recv, mv_send, mv_recv, ag_send, ag_recv, far_send, far_recv, row_send, row_recv,
    here, ready, open_sem,
    *, slots, steps, heads, n_dp, n_t, parity,
):
    g, t = lax.axis_index("dp"), lax.axis_index("tensor")
    up, down = lax.rem(g + 1, n_dp), lax.rem(g + n_dp - 1, n_dp)
    rows = slots * steps
    is_src = lax.rem(g, 2) == parity
    is_dst = jnp.logical_not(is_src)
    far = parity == 1
    place16 = lax.rem(g, 16)
    far_src_first = jnp.logical_and(is_src, place16 == 7)
    far_dst_last = jnp.logical_and(is_dst, place16 == 8)
    far_src_last = jnp.logical_and(is_src, place16 == 15)
    far_dst_first = jnp.logical_and(is_dst, place16 == 0)
    near = jnp.logical_or(
        jnp.logical_and(is_src, jnp.logical_and(place16 != 7, place16 != 15)),
        jnp.logical_and(is_dst, jnp.logical_and(place16 != 8, place16 != 0)),
    )
    relays = jnp.logical_and(far_src_first, t == 0)
    owner = jnp.where(g == 0, 1, 0)
    adds = jnp.logical_and(far_dst_first, t == owner)
    owner_up = jnp.where(up == 0, 1, 0)
    relay_of_dst = lax.rem(g + n_dp - 9, n_dp)
    relay_of_src = lax.rem(g + n_dp - 8, n_dp)
    relay_dst = lax.rem(g + 9, n_dp)
    relay_src = lax.rem(g + 8, n_dp)

    def when(*conditions):
        return pl.when(functools.reduce(jnp.logical_and, conditions))

    pairs = [
        (mig_hbm, mig), (query_hbm, query), (new_keys_hbm, new_keys),
        (new_values_hbm, new_values), (lengths_hbm, lengths), (finished_hbm, finished),
    ]
    pairs += [(keys_hbm.at[r], keys.at[r]) for r in range(slots)]
    pairs += [(values_hbm.at[r], values.at[r]) for r in range(slots)]
    pairs += [
        (weight_hbm.at[:, pl.ds(256 * c, 256)], weight.at[:, pl.ds(256 * c, 256)])
        for c in range(10)
    ]
    loads = [
        pltpu.make_async_copy(src, dst, load_sem.at[i]) for i, (src, dst) in enumerate(pairs)
    ]
    for load in loads:
        load.start()
    key_loads, value_loads = loads[6 : 6 + slots], loads[6 + slots : 6 + 2 * slots]
    weight_loads = loads[6 + 2 * slots :]

    barrier = pltpu.get_barrier_semaphore()

    def greet(group, other):
        pl.semaphore_signal(barrier, inc=1, device_id=(group, other), device_id_type=MESH)

    def tell(sem, group, other):
        pl.semaphore_signal(sem, inc=1, device_id=(group, other), device_id_type=MESH)

    near_src = jnp.logical_and(is_src, near) if far else is_src
    near_dst = jnp.logical_and(is_dst, near) if far else is_dst

    def rank_of(group, other):
        return jnp.where(jnp.logical_and(group == 0, other == 0), n_t, other)

    rank = rank_of(g, t)
    last = rank == n_t
    before_last = jnp.logical_and(g == 0, t > 0)

    for j in range(n_t):

        @when(rank_of(g, j) > rank)
        def _():
            greet(g, j)

        @when(near_src, j >= rank)
        def _():
            greet(up, j)

        @when(near_dst, rank_of(down, j) >= t)
        def _():
            greet(down, j)

    if far:

        @when(far_src_first)
        def _():
            for j in range(n_t):
                greet(up, j)

        @when(adds)
        def _():
            for j in range(n_t):
                greet(down, j)

        @when(relays)
        def _():
            for j in range(n_t):
                greet(relay_dst, j)
                greet(relay_src, j)

        greeted = jnp.where(
            near, t + 1,
            jnp.where(
                far_dst_last, n_t,
                jnp.where(far_src_last, 2, jnp.where(far_dst_first, 1, 0)),
            ),
        )
        greeted = jnp.where(last, n_t, t + greeted)
        fewer = before_last
    else:
        greeted = jnp.where(last, 2 * n_t - 1, 2 * t + 1)
        fewer = jnp.logical_or(before_last, g == 1)
    greeted = greeted - jnp.where(fewer, 1, 0)

    @when(greeted > 0)
    def _():
        pl.semaphore_wait(barrier, greeted)


    for j in range(n_t):

        @when(rank_of(g, j) < rank)
        def _():
            tell(here.at[t], g, j)

        @when(near_dst, rank_of(down, j) < t, t != n_t - 1)
        def _():
            tell(ready.at[t], down, j)

    ask_later = jnp.logical_and(g == 1, t == 0)
    if far:

        @when(far_dst_last, t != n_t - 1)
        def _():
            for j in range(n_t):
                tell(ready.at[t], down, j)

        @when(far_src_last)
        def _():
            tell(open_sem.at[t], relay_of_src, 0)

    else:

        @when(last)
        def _():
            tell(ready.at[0], up, 0)

    def ask_copy(group, other):
        return pltpu.make_async_remote_copy(
            ask, asked, ask_send, ask_recv, device_id=(group, other), device_id_type=MESH
        )

    def relay_copy(slot, group):
        return pltpu.make_async_remote_copy(
            ask, relay.at[slot], ask_send, relay_recv.at[slot],
            device_id=(group, 0), device_id_type=MESH,
        )

    def pass_copy(j):
        return pltpu.make_async_remote_copy(
            relay.at[j], asked, relay_send.at[j], ask_recv,
            device_id=(relay_src, j), device_id_type=MESH,
        )

    adder = list(range(n_t - 1)) + [HELPER]
    side = [0] * (n_t - 1) + [1]

    def rs_copy(c, slot):
        return pltpu.make_async_remote_copy(
            part.at[c], reduced.at[side[c], slot], rs_send.at[c], rs_recv.at[side[c], slot],
            device_id=(g, adder[c]), device_id_type=MESH,
        )

    def mv_copy(c, slot):
        return pltpu.make_async_remote_copy(
            moved_part.at[c], moved_in.at[side[c], slot], mv_send.at[c],
            mv_recv.at[side[c], slot], device_id=(up, adder[c]), device_id_type=MESH,
        )

    def far_copy(slot):
        return pltpu.make_async_remote_copy(
            far_part, far_in.at[slot], far_send, far_recv.at[slot],
            device_id=(up, owner_up), device_id_type=MESH,
        )

    tree = {0: (1, 2, 4), 2: (3,), 4: (5, 6), 6: (7,)}

    def place_in_tree(j):
        return jnp.where(j == owner, 0, jnp.where(j == 0, owner, j))

    my_place = place_in_tree(t)

    def row_copy(j):
        return pltpu.make_async_remote_copy(
            far_row, far_row, row_send.at[j], row_recv, device_id=(g, j), device_id_type=MESH
        )

    def ag_copy(k, j, c):
        return pltpu.make_async_remote_copy(
            chunk.at[k], gathered.at[c], ag_send.at[k, j], ag_recv.at[c],
            device_id=(g, j), device_id_type=MESH,
        )

    for load in loads[:6]:
        load.wait()
    sending = mig[0:1, :] == g
    arriving = mig[1:2, :] == g
    has_send = jnp.sum(sending.astype(jnp.int32)) > 0
    has_arrival = jnp.sum(arriving.astype(jnp.int32)) > 0
    sent_row = jnp.sum(jnp.where(sending, mig[2:3, :], 0))
    arrival_slot = jnp.sum(jnp.where(arriving, mig[3:4, :], 0))

    def flat(ref):
        return jnp.concatenate([ref[s].astype(F32) for s in range(steps)], axis=0)

    i, j = grid_ids((rows + steps, rows))
    slot = jnp.where(i < rows, i // steps, arrival_slot)
    order = one_hot(j == lax.rem(i, steps) * slots + slot)
    by_slot = dot(order, flat(query).astype(BF16))
    fresh = jnp.concatenate([flat(new_keys), flat(new_values)], axis=1).astype(BF16)
    fresh_by_slot = dot(order, fresh)
    ask[0 : heads * steps, :] = stack_heads(by_slot[rows:], heads).astype(BF16)
    ask[heads * steps :, :] = stack_heads(fresh_by_slot[rows:], 2).astype(BF16)

    if far:

        @when(is_dst, jnp.logical_not(far_dst_first))
        def _():
            ask_copy(down, t).start()

        @when(far_dst_first)
        def _():
            relay_copy(t, relay_of_dst).start()

    else:

        @when(is_dst, jnp.logical_not(ask_later))
        def _():
            ask_copy(down, t).start()

    zeros = jnp.zeros((16 - steps, HD), F32)

    def pad(x):
        return jnp.concatenate([x, zeros], axis=0).astype(BF16)

    attended = []
    for load in key_loads + value_loads:
        load.wait()
    for r in range(slots):
        mine = slice(r * steps, (r + 1) * steps)
        mixed = attend(
            stack_heads(by_slot[mine], heads).astype(BF16),
            keys[r], values[r],
            pad(fresh_by_slot[mine, :HD]), pad(fresh_by_slot[mine, HD:]),
            lengths[r] * BLOCK, steps, heads,
        )
        stays = jnp.logical_and(
            finished[r] == 0, jnp.logical_not(jnp.logical_and(has_send, sent_row == r))
        )
        attended.append(jnp.where(stays, mixed, 0.0))
    attended = jnp.concatenate(attended, axis=0).astype(BF16)
    i, j = grid_ids((rows, rows))
    to_steps = one_hot(j == lax.rem(i, slots) * steps + i // slots)
    attended = dot(to_steps, attended).astype(BF16)

    half = rows // 2

    def put_part(c, block):
        block = block.astype(BF16)
        for k in range(2):
            for h in range(2):
                piece = block[h * half : (h + 1) * half, k * LANES : (k + 1) * LANES]
                if c < 8:
                    part[c, 2 * k + h] = piece
                else:
                    part[2 * (2 * (c - 8) + k) + h, 4] = piece

    def put_moved(c, block):
        piece = jnp.concatenate([block[:, :LANES], block[:, LANES:]], axis=0).astype(BF16)
        if far:
            far_part[c] = piece
        if c < 8:
            moved_part[c, 0] = piece
        else:
            for j in range(4):
                moved_part[4 * (c - 8) + j, 1] = piece

    def columns(c):
        return weight[:, 256 * c : 256 * (c + 1)]

    def attend_moved():
        ask_copy(g, t).wait_recv()
        asked_fresh = asked[heads * steps :, :].astype(F32)
        moved = attend(
            asked[0 : heads * steps, :],
            keys[sent_row], values[sent_row],
            pad(asked_fresh[:steps]), pad(asked_fresh[steps:]),
            lengths[sent_row] * BLOCK, steps, heads,
        )
        return jnp.where(has_send, moved, 0.0).astype(BF16)

    def send_all(parts, moved):
        for c in reversed(range(n_t)):
            o = adder[c]
            if moved:

                @when(near_src, o <= rank)
                def _():
                    mv_copy(c, t).start()

            if parts:

                @when(rank_of(g, o) < rank)
                def _():
                    rs_copy(c, t).start()

        for o in list(range(1, n_t - 1)) + [0]:
            own = [c for c in range(n_t) if adder[c] == o]
            if moved:

                @when(near_src, o > rank)
                def _():
                    pl.semaphore_wait(ready.at[o], 1)
                    for c in own:
                        mv_copy(c, t).start()

            if parts:

                @when(rank_of(g, o) > rank)
                def _():
                    pl.semaphore_wait(here.at[o], 1)
                    for c in own:
                        rs_copy(c, t).start()

        if moved and far:

            @when(far_src_first)
            def _():
                for o in range(n_t - 1):
                    pl.semaphore_wait(ready.at[o], 1)
                    for c in range(n_t):
                        if adder[c] == o:
                            mv_copy(c, t).start()

            @when(far_src_last)
            def _():
                far_copy(t).start()

    if far:
        for c in range(10):
            weight_loads[c].wait()
            put_part(c, dot(attended, columns(c)))
        send_all(True, False)

        @when(relays)
        def _():
            for j in range(n_t):
                pl.semaphore_wait(open_sem.at[j], 1)
                relay_copy(j, g).wait_recv()
                pass_copy(j).start()

        @when(is_src)
        def _():
            moved = attend_moved()
            for c in range(10):
                put_moved(c, dot(moved, columns(c)))
            send_all(False, True)

    else:

        @when(is_src)
        def _():
            both = jnp.concatenate([attended.astype(F32), attend_moved().astype(F32)], axis=0)
            both = both.astype(BF16)
            for c in range(10):
                weight_loads[c].wait()
                block = dot(both, columns(c))
                put_part(c, block[:rows])
                put_moved(c, block[rows:])
            send_all(True, True)

        @when(ask_later)
        def _():
            pl.semaphore_wait(ready.at[0], 1)
            ask_copy(down, t).start()

        @when(is_dst)
        def _():
            for c in range(10):
                weight_loads[c].wait()
                put_part(c, dot(attended, columns(c)))
            send_all(True, False)

    i, j = grid_ids((rows, steps))
    place = one_hot(jnp.logical_and(lax.rem(i, slots) == arrival_slot, i // slots == j))
    takes_moved = jnp.logical_and(is_dst, jnp.logical_not(far_dst_first)) if far else is_dst

    def finish(k, c, sender):
        reduced[k, t] = part[c]
        for j in range(n_t):

            @when(j != t)
            def _():
                rs_copy(sender, j).wait_recv()

        acc = reduced[k, 0].astype(F32)
        for j in range(1, n_t):
            acc = acc + reduced[k, j].astype(F32)
        total[...] = acc

        @when(takes_moved)
        def _():
            for j in range(n_t):
                mv_copy(sender, j).wait_recv()
            arrived = moved_in[k, 0].astype(F32)
            for j in range(1, n_t):
                arrived = arrived + moved_in[k, j].astype(F32)
            arrived = jnp.where(has_arrival, arrived, 0.0).astype(BF16)
            lo = dot(place, arrived[0, :steps])
            hi = dot(place, arrived[0, steps:])
            extra = dot(
                place,
                jnp.where(lax.rem(c // 2, 2) == 0, arrived[1, :steps], arrived[1, steps:]),
            )
            extra = jnp.where(lax.rem(c, 2) == 0, extra[:half], extra[half:])
            total[0] += lo[:half]
            total[1] += lo[half:]
            total[2] += hi[:half]
            total[3] += hi[half:]
            total[4] += extra

        chunk[k] = total[...].astype(BF16)
        gathered[c] = chunk[k]
        for j in range(n_t - 1):

            @when(j != t)
            def _():
                ag_copy(k, j, c).start()

    @when(t == HELPER)
    def _():
        finish(1, n_t - 1, n_t - 1)

    @when(t < n_t - 1)
    def _():
        finish(0, t, 0)

    @when(rank < n_t - 1)
    def _():
        pl.semaphore_wait(here.at[n_t - 1], 1)

    @when(t < n_t - 1)
    def _():
        ag_copy(0, n_t - 1, t).start()

    @when(t == HELPER)
    def _():
        ag_copy(1, n_t - 1, n_t - 1).start()

    for c in range(n_t):

        @when(t != adder[c])
        def _():
            ag_copy(0, 0, c).wait_recv()

    for j in range(n_t):
        for k in range(2):
            for h in range(2):
                out[h * half : (h + 1) * half, (2 * j + k) * LANES : (2 * j + k + 1) * LANES] = (
                    gathered[j, 2 * k + h]
                )
        tile = 2 * n_t + j // 2
        h = j % 2
        out[h * half : (h + 1) * half, tile * LANES : (tile + 1) * LANES] = gathered[j, 4]

    if far:

        @when(adds)
        def _():
            for j in range(n_t):
                far_copy(j).wait_recv()
            arrived = far_in[0].astype(F32)
            for j in range(1, n_t):
                arrived = arrived + far_in[j].astype(F32)
            far_row[...] = jnp.where(has_arrival, arrived, 0.0).astype(BF16)

        @when(far_dst_first, jnp.logical_not(adds))
        def _():
            row_copy(0).wait_recv()

        for spot, followers in tree.items():

            @when(far_dst_first, my_place == spot)
            def _():
                for j in followers:
                    row_copy(place_in_tree(j)).start()

        @when(far_dst_first)
        def _():
            for c in range(10):
                pair = jnp.concatenate([far_row[c, :steps], far_row[c, steps:]], axis=1)
                out[:, 256 * c : 256 * (c + 1)] += dot(place, pair).astype(BF16)

        for spot, followers in tree.items():

            @when(far_dst_first, my_place == spot)
            def _():
                for j in followers:
                    row_copy(place_in_tree(j)).wait_send()

    for j in range(n_t):

        @when(t != adder[j])
        def _():
            rs_copy(j, t).wait_send()

        @when(t != j, t < n_t - 1)
        def _():
            ag_copy(0, j, t).wait_send()

        @when(t != j, t == HELPER)
        def _():
            ag_copy(1, j, n_t - 1).wait_send()

    if far:

        @when(far_src_last)
        def _():
            far_copy(t).wait_send()

    @when(is_src, jnp.logical_not(far_src_last) if far else True)
    def _():
        for j in range(n_t):
            mv_copy(j, t).wait_send()

    @pl.when(is_dst)
    def _():
        ask_copy(down, t).wait_send()

    if far:

        @pl.when(relays)
        def _():
            for j in range(n_t):
                pass_copy(j).wait_send()


def parity_kernel(mig_hbm, out, mig, sem):
    load = pltpu.make_async_copy(mig_hbm, mig, sem)
    load.start()
    load.wait()
    out[0] = lax.rem(mig[0, 0], 2)


def source_parity(moves):
    return pl.pallas_call(
        parity_kernel,
        out_shape=jax.ShapeDtypeStruct((1,), jnp.int32),
        in_specs=[pl.BlockSpec(memory_space=pltpu.HBM)],
        out_specs=pl.BlockSpec(memory_space=pltpu.SMEM),
        scratch_shapes=[pltpu.SMEM(moves.shape, jnp.int32), pltpu.SemaphoreType.DMA],
    )(moves)[0]


def project(parity, n_dp, n_t, *operands):
    lengths, finished, moves, queries, new_keys, new_values, keys, values, weight = operands
    steps, slots, width = queries.shape
    features = weight.shape[1]
    heads = width // HD
    rows = steps * slots
    dma = pltpu.SemaphoreType.DMA
    regular = pltpu.SemaphoreType.REGULAR
    asks = ((heads + 2) * steps, HD)
    pieces = (n_t, 5, rows // 2, LANES)
    moved = (n_t, 2, 2 * steps, LANES)
    far = (features // (2 * LANES), 2 * steps, LANES)
    return pl.pallas_call(
        functools.partial(
            kernel, slots=slots, steps=steps, heads=heads, n_dp=n_dp, n_t=n_t, parity=parity
        ),
        out_shape=jax.ShapeDtypeStruct((rows, features), BF16),
        in_specs=[pl.BlockSpec(memory_space=pltpu.HBM)] * 9,
        out_specs=pl.BlockSpec(memory_space=pltpu.VMEM),
        scratch_shapes=[
            pltpu.SMEM(lengths.shape, jnp.int32),
            pltpu.SMEM(finished.shape, jnp.int32),
            pltpu.VMEM(moves.shape, jnp.int32),
            pltpu.VMEM(queries.shape, BF16),
            pltpu.VMEM(new_keys.shape, BF16),
            pltpu.VMEM(new_values.shape, BF16),
            pltpu.VMEM(keys.shape, BF16),
            pltpu.VMEM(values.shape, BF16),
            pltpu.VMEM(weight.shape, BF16),
            pltpu.VMEM(asks, BF16),
            pltpu.VMEM(asks, BF16),
            pltpu.VMEM((n_t,) + asks, BF16),
            pltpu.VMEM(pieces, BF16),
            pltpu.VMEM((2,) + pieces, BF16),
            pltpu.VMEM(moved, BF16),
            pltpu.VMEM((2,) + moved, BF16),
            pltpu.VMEM(far, BF16),
            pltpu.VMEM((n_t,) + far, BF16),
            pltpu.VMEM(far, BF16),
            pltpu.VMEM(pieces[1:], F32),
            pltpu.VMEM((2,) + pieces[1:], BF16),
            pltpu.VMEM(pieces, BF16),
            dma((6 + 2 * slots + 10,)), dma, dma, dma((n_t,)), dma((n_t,)),
            dma((n_t,)), dma((2, n_t)), dma((n_t,)), dma((2, n_t)), dma((2, n_t)), dma((n_t,)),
            dma, dma((n_t,)), dma((n_t,)), dma,
            regular((n_t,)), regular((n_t,)), regular((n_t,)),
        ],
        compiler_params=pltpu.CompilerParams(
            collective_id=parity, has_side_effects=True, vmem_limit_bytes=48 << 20
        ),
    )(*operands)


def per_device(n_dp, n_t, cache_keys, cache_values, lengths, finished, migrations, queries,
               new_keys, new_values, out_weight):
    steps, slots, _ = queries.shape
    moves = migrations.T
    result = lax.cond(
        source_parity(moves) == 0,
        functools.partial(project, 0, n_dp, n_t),
        functools.partial(project, 1, n_dp, n_t),
        lengths, finished, moves, queries, new_keys, new_values,
        cache_keys, cache_values, out_weight,
    )
    return result.reshape(steps, slots, out_weight.shape[1])


def solution(mesh):
    sizes = dict(zip(mesh.axis_names, mesh.devices.shape))
    return jax.shard_map(
        functools.partial(per_device, sizes["dp"], sizes["tensor"]),
        mesh=mesh,
        in_specs=(
            P("dp", None, "tensor"),
            P("dp", None, "tensor"),
            P("dp"),
            P("dp"),
            P(),
            P(None, "dp", "tensor"),
            P(None, "dp", "tensor"),
            P(None, "dp", "tensor"),
            P("tensor", None),
        ),
        out_specs=P(None, "dp", None),
        check_vma=False,
    )
```

```python
import functools

import jax
import jax.numpy as jnp
from jax import lax
from jax.experimental import pallas as pl
from jax.experimental.pallas import tpu as pltpu
from jax.sharding import PartitionSpec as P

HD = 128
BLOCK = 512
LANES = 128
BLOCK_ORDER = (8, 9, 7, 6, 5, 4, 3, 2, 1, 0)
MESH = pl.DeviceIdType.MESH
F32 = jnp.float32
BF16 = jnp.bfloat16


def one_hot(mask):
    return jnp.where(mask, 1.0, 0.0).astype(BF16)


def grid_ids(shape):
    return (
        lax.broadcasted_iota(jnp.int32, shape, 0),
        lax.broadcasted_iota(jnp.int32, shape, 1),
    )


def dot(a, b):
    return lax.dot_general(a, b, (((1,), (0,)), ((), ())), preferred_element_type=F32)


def dot_t(a, b):
    return lax.dot_general(a, b, (((1,), (1,)), ((), ())), preferred_element_type=F32)


def stack_heads(rows, heads):
    return jnp.concatenate([rows[:, h * HD : (h + 1) * HD] for h in range(heads)], axis=0)


def attend(query, keys, values, fresh_keys, fresh_values, limit, steps, heads):
    scale = 1.0 / HD**0.5
    scores = dot_t(query, keys) * scale
    fresh = dot_t(query, fresh_keys) * scale
    _, position = grid_ids(scores.shape)
    scores = jnp.where(position < limit, scores, -1e30)
    row, token = grid_ids(fresh.shape)
    fresh = jnp.where(token <= lax.rem(row, steps), fresh, -1e30)
    peak = jnp.maximum(
        jnp.max(scores, axis=1, keepdims=True), jnp.max(fresh, axis=1, keepdims=True)
    )
    weights = jnp.exp(scores - peak)
    fresh_weights = jnp.exp(fresh - peak)
    total = jnp.sum(weights, axis=1, keepdims=True) + jnp.sum(fresh_weights, axis=1, keepdims=True)
    mixed = dot(weights.astype(BF16), values) + dot(fresh_weights.astype(BF16), fresh_values)
    mixed = mixed / total
    return jnp.concatenate([mixed[h * steps : (h + 1) * steps] for h in range(heads)], axis=1)


def kernel(
    lengths_hbm, finished_hbm, mig_hbm, query_hbm, new_keys_hbm, new_values_hbm,
    keys_hbm, values_hbm, weight_hbm,
    out,
    lengths, finished, mig, query, new_keys, new_values, keys, values, weight,
    ask, asked, relay, part, reduced, moved_part, moved_in, far_part, far_in, far_row, back, returned,
    rows_in, total, chunk,
    gathered,
    load_sem, ask_send, ask_recv, relay_send, relay_recv,
    rs_send, rs_recv, mv_send, mv_recv, ag_send, ag_recv, far_send, far_recv, row_send, row_recv, back_send, back_recv,
    here, ready, open_sem,
    *, slots, steps, heads, n_dp, n_t, parity,
):
    g, t = lax.axis_index("dp"), lax.axis_index("tensor")
    up, down = lax.rem(g + 1, n_dp), lax.rem(g + n_dp - 1, n_dp)
    rows = slots * steps
    is_src = lax.rem(g, 2) == parity
    is_dst = jnp.logical_not(is_src)
    far = parity == 1
    place16 = lax.rem(g, 16)
    far_src_first = jnp.logical_and(is_src, place16 == 7)
    far_dst_last = jnp.logical_and(is_dst, place16 == 8)
    far_src_last = jnp.logical_and(is_src, place16 == 15)
    far_dst_first = jnp.logical_and(is_dst, place16 == 0)
    near = jnp.logical_or(
        jnp.logical_and(is_src, jnp.logical_and(place16 != 7, place16 != 15)),
        jnp.logical_and(is_dst, jnp.logical_and(place16 != 8, place16 != 0)),
    )
    relays = jnp.logical_and(far_src_first, t == 0)
    owner = jnp.where(g == 0, 1, 0)
    adds = jnp.logical_and(far_dst_first, t == owner)
    owner_up = jnp.where(up == 0, 1, 0)
    relay_of_dst = lax.rem(g + n_dp - 9, n_dp)
    relay_of_src = lax.rem(g + n_dp - 8, n_dp)
    relay_dst = lax.rem(g + 9, n_dp)
    relay_src = lax.rem(g + 8, n_dp)

    def when(*conditions):
        return pl.when(functools.reduce(jnp.logical_and, conditions))

    pairs = [
        (mig_hbm, mig), (query_hbm, query), (new_keys_hbm, new_keys),
        (new_values_hbm, new_values), (lengths_hbm, lengths), (finished_hbm, finished),
    ]
    pairs += [(keys_hbm.at[r], keys.at[r]) for r in range(slots)]
    pairs += [(values_hbm.at[r], values.at[r]) for r in range(slots)]
    pairs += [
        (weight_hbm.at[:, pl.ds(256 * c, 256)], weight.at[:, pl.ds(256 * c, 256)])
        for c in BLOCK_ORDER
    ]
    loads = [
        pltpu.make_async_copy(src, dst, load_sem.at[i]) for i, (src, dst) in enumerate(pairs)
    ]
    for load in loads:
        load.start()
    key_loads, value_loads = loads[6 : 6 + slots], loads[6 + slots : 6 + 2 * slots]
    weight_loads = loads[6 + 2 * slots :]

    barrier = pltpu.get_barrier_semaphore()

    def greet(group, other):
        pl.semaphore_signal(barrier, inc=1, device_id=(group, other), device_id_type=MESH)

    def tell(sem, group, other):
        pl.semaphore_signal(sem, inc=1, device_id=(group, other), device_id_type=MESH)

    near_src = jnp.logical_and(is_src, near) if far else is_src
    near_dst = jnp.logical_and(is_dst, near) if far else is_dst

    def rank_of(group, other):
        return jnp.where(jnp.logical_and(group == 0, other == 0), n_t, other)

    rank = rank_of(g, t)
    last = rank == n_t
    before_last = jnp.logical_and(g == 0, t > 0)

    for j in range(n_t):

        @when(rank_of(g, j) > rank)
        def _():
            greet(g, j)

        @when(near_src, j >= rank)
        def _():
            greet(up, j)

        @when(near_dst, rank_of(down, j) >= t)
        def _():
            greet(down, j)

    if far:

        @when(far_src_first)
        def _():
            for j in range(n_t):
                greet(up, j)

        @when(adds)
        def _():
            for j in range(n_t):
                greet(down, j)

        @when(relays)
        def _():
            for j in range(n_t):
                greet(relay_dst, j)
                greet(relay_src, j)

        greeted = jnp.where(
            near, t + 1,
            jnp.where(
                far_dst_last, n_t,
                jnp.where(far_src_last, 2, jnp.where(far_dst_first, 1, 0)),
            ),
        )
        greeted = jnp.where(last, n_t, t + greeted)
        fewer = before_last
    else:
        greeted = jnp.where(last, 2 * n_t - 1, 2 * t + 1)
        fewer = jnp.logical_or(before_last, g == 1)
    greeted = greeted - jnp.where(fewer, 1, 0)

    @when(greeted > 0)
    def _():
        pl.semaphore_wait(barrier, greeted)


    for j in range(n_t):

        @when(rank_of(g, j) < rank)
        def _():
            tell(here.at[t], g, j)

        if far:

            @when(near_dst, rank_of(down, j) < t, t != n_t - 1)
            def _():
                tell(ready.at[t], down, j)

    ask_later = jnp.logical_and(g == 1, t == 0)
    if far:

        @when(far_dst_last, t != n_t - 1)
        def _():
            for j in range(n_t):
                tell(ready.at[t], down, j)

        @when(far_src_last)
        def _():
            tell(open_sem.at[t], relay_of_src, 0)

    else:

        @when(last)
        def _():
            tell(ready.at[0], up, 0)

    def ask_copy(group, other):
        return pltpu.make_async_remote_copy(
            ask, asked, ask_send, ask_recv, device_id=(group, other), device_id_type=MESH
        )

    def relay_copy(slot, group):
        return pltpu.make_async_remote_copy(
            ask, relay.at[slot], ask_send, relay_recv.at[slot],
            device_id=(group, 0), device_id_type=MESH,
        )

    def pass_copy(j):
        return pltpu.make_async_remote_copy(
            relay.at[j], asked, relay_send.at[j], ask_recv,
            device_id=(relay_src, j), device_id_type=MESH,
        )

    adders = n_t - 1 if far else n_t

    def rs_copy(c, slot):
        return pltpu.make_async_remote_copy(
            part.at[c], reduced.at[slot], rs_send.at[c], rs_recv.at[slot],
            device_id=(g, c), device_id_type=MESH,
        )

    def mv_copy(c, slot):
        return pltpu.make_async_remote_copy(
            moved_part.at[c], moved_in.at[slot], mv_send.at[c], mv_recv.at[slot],
            device_id=(up, c), device_id_type=MESH,
        )

    def back_copy(group):
        return pltpu.make_async_remote_copy(
            back, returned, back_send, back_recv, device_id=(group, t), device_id_type=MESH
        )

    def far_copy(slot):
        return pltpu.make_async_remote_copy(
            far_part, far_in.at[slot], far_send, far_recv.at[slot],
            device_id=(up, owner_up), device_id_type=MESH,
        )

    tree = {0: (1, 2, 4), 2: (3,), 4: (5, 6), 6: (7,)}

    def place_in_tree(j):
        return jnp.where(j == owner, 0, jnp.where(j == 0, owner, j))

    my_place = place_in_tree(t)

    def row_copy(j):
        return pltpu.make_async_remote_copy(
            far_row, far_row, row_send.at[j], row_recv, device_id=(g, j), device_id_type=MESH
        )

    def ag_copy(j, c):
        return pltpu.make_async_remote_copy(
            chunk, gathered.at[c], ag_send.at[j], ag_recv.at[c],
            device_id=(g, j), device_id_type=MESH,
        )

    for load in loads[:6]:
        load.wait()
    sending = mig[0:1, :] == g
    arriving = mig[1:2, :] == g
    has_send = jnp.sum(sending.astype(jnp.int32)) > 0
    has_arrival = jnp.sum(arriving.astype(jnp.int32)) > 0
    sent_row = jnp.sum(jnp.where(sending, mig[2:3, :], 0))
    arrival_slot = jnp.sum(jnp.where(arriving, mig[3:4, :], 0))

    def flat(ref):
        return jnp.concatenate([ref[s].astype(F32) for s in range(steps)], axis=0)

    i, j = grid_ids((rows + steps, rows))
    slot = jnp.where(i < rows, i // steps, arrival_slot)
    order = one_hot(j == lax.rem(i, steps) * slots + slot)
    by_slot = dot(order, flat(query).astype(BF16))
    fresh = jnp.concatenate([flat(new_keys), flat(new_values)], axis=1).astype(BF16)
    fresh_by_slot = dot(order, fresh)
    ask[0 : heads * steps, :] = stack_heads(by_slot[rows:], heads).astype(BF16)
    ask[heads * steps :, :] = stack_heads(fresh_by_slot[rows:], 2).astype(BF16)

    if far:

        @when(is_dst, jnp.logical_not(far_dst_first))
        def _():
            ask_copy(down, t).start()

        @when(far_dst_first)
        def _():
            relay_copy(t, relay_of_dst).start()

    else:

        @when(is_dst, jnp.logical_not(ask_later))
        def _():
            ask_copy(down, t).start()

    zeros = jnp.zeros((16 - steps, HD), F32)

    def pad(x):
        return jnp.concatenate([x, zeros], axis=0).astype(BF16)

    def attend_moved():
        ask_copy(g, t).wait_recv()
        asked_fresh = asked[heads * steps :, :].astype(F32)
        moved = attend(
            asked[0 : heads * steps, :],
            keys[sent_row], values[sent_row],
            pad(asked_fresh[:steps]), pad(asked_fresh[steps:]),
            lengths[sent_row] * BLOCK, steps, heads,
        )
        return jnp.where(has_send, moved, 0.0)

    attended = []
    for load in key_loads + value_loads:
        load.wait()
    for r in range(slots):
        if r in (0, slots // 2) and not far:
            @when(is_src, last if r == 0 else jnp.logical_not(last))
            def _():
                back[...] = stack_heads(attend_moved(), heads).astype(BF16)
                back_copy(up).start()

        mine = slice(r * steps, (r + 1) * steps)
        mixed = attend(
            stack_heads(by_slot[mine], heads).astype(BF16),
            keys[r], values[r],
            pad(fresh_by_slot[mine, :HD]), pad(fresh_by_slot[mine, HD:]),
            lengths[r] * BLOCK, steps, heads,
        )
        stays = jnp.logical_and(
            finished[r] == 0, jnp.logical_not(jnp.logical_and(has_send, sent_row == r))
        )
        attended.append(jnp.where(stays, mixed, 0.0))
    attended = jnp.concatenate(attended, axis=0)
    if not far:
        rows_in[...] = attended

        @when(ask_later)
        def _():
            pl.semaphore_wait(ready.at[0], 1)
            ask_copy(down, t).start()

        @when(is_dst)
        def _():
            back_copy(down).wait_recv()
            row = returned[...].astype(F32)
            row = jnp.concatenate([row[h * steps : (h + 1) * steps] for h in range(heads)], axis=1)
            for r in range(slots):
                mine = slice(r * steps, (r + 1) * steps)
                here_now = jnp.logical_and(has_arrival, arrival_slot == r)
                rows_in[mine, :] = jnp.where(here_now, row, rows_in[mine, :])

        attended = rows_in[...]
    attended = attended.astype(BF16)
    i, j = grid_ids((rows, rows))
    to_steps = one_hot(j == lax.rem(i, slots) * steps + i // slots)
    attended = dot(to_steps, attended).astype(BF16)

    half = rows // 2

    def home_of(c, k, h):
        if c < adders:
            return c, 2 * k + h
        if far and c == adders:
            return 2 * k + h, 5
        n = 2 * (2 * (c - n_t) + k) + h
        return (n, 4) if n < adders else (4, 5)

    def put_part(c, block):
        block = block.astype(BF16)
        for k in range(2):
            for h in range(2):
                piece = block[h * half : (h + 1) * half, k * LANES : (k + 1) * LANES]
                n, m = home_of(c, k, h)
                part[n, m] = piece

    for c in (5, 6) if far else ():
        part[c, 5] = jnp.zeros(part.shape[2:], BF16)

    def put_moved(c, block):
        piece = jnp.concatenate([block[:, :LANES], block[:, LANES:]], axis=0).astype(BF16)
        if far:
            far_part[c] = piece
        if c < adders:
            moved_part[c, 0] = piece
        elif c == adders:
            for j in range(adders):
                moved_part[j, 2] = piece
        else:
            for j in range(4 * (c - 8), min(4 * (c - 7), adders)):
                moved_part[j, 1] = piece

    def columns(c):
        return weight[:, 256 * c : 256 * (c + 1)]

    def send_all(parts, moved):
        for c in reversed(range(adders)):
            if moved:

                @when(near_src, c <= rank)
                def _():
                    mv_copy(c, t).start()

        for c in list(range(1, adders)) + [0]:
            if moved:

                @when(near_src, c > rank)
                def _():
                    pl.semaphore_wait(ready.at[c], 1)
                    mv_copy(c, t).start()

            if parts:

                @when(rank_of(g, c) > rank)
                def _():
                    pl.semaphore_wait(here.at[c], 1)
                    rs_copy(c, t).start()

        if moved and far:

            @when(far_src_first)
            def _():
                for c in range(adders):
                    pl.semaphore_wait(ready.at[c], 1)
                    mv_copy(c, t).start()

            @when(far_src_last)
            def _():
                far_copy(t).start()

    for load, c in zip(weight_loads, BLOCK_ORDER):
        load.wait()
        put_part(c, dot(attended, columns(c)))
        if c < adders:
            @when(rank_of(g, c) < rank)
            def _():
                rs_copy(c, t).start()

    send_all(True, False)

    if far:

        @when(relays)
        def _():
            for j in range(n_t):
                pl.semaphore_wait(open_sem.at[j], 1)
                relay_copy(j, g).wait_recv()
                pass_copy(j).start()

        @when(is_src)
        def _():
            moved = attend_moved().astype(BF16)
            for c in range(10):
                put_moved(c, dot(moved, columns(c)))
            send_all(False, True)

    i, j = grid_ids((rows, steps))
    place = one_hot(jnp.logical_and(lax.rem(i, slots) == arrival_slot, i // slots == j))

    @when(t < adders)
    def _():
        reduced[t] = part[t]
        for j in range(n_t):

            @when(j != t)
            def _():
                rs_copy(0, j).wait_recv()

        acc = reduced[0].astype(F32)
        for j in range(1, n_t):
            acc = acc + reduced[j].astype(F32)
        total[...] = acc

        def add_moved():
            for j in range(n_t):
                mv_copy(0, j).wait_recv()
            arrived = moved_in[0].astype(F32)
            for j in range(1, n_t):
                arrived = arrived + moved_in[j].astype(F32)
            arrived = jnp.where(has_arrival, arrived, 0.0).astype(BF16)
            odd = lax.rem(t, 2) == 1
            lo = dot(place, arrived[0, :steps])
            hi = dot(place, arrived[0, steps:])
            fifth = jnp.where(lax.rem(t // 2, 2) == 0, arrived[1, :steps], arrived[1, steps:])
            fifth = dot(place, fifth)
            sixth = jnp.where(t < 2, arrived[2, :steps], arrived[2, steps:])
            sixth = dot(place, jnp.where(t == 4, arrived[1, steps:], sixth))
            total[0] += lo[:half]
            total[1] += lo[half:]
            total[2] += hi[:half]
            total[3] += hi[half:]
            total[4] += jnp.where(odd, fifth[half:], fifth[:half])
            total[5] += jnp.where(jnp.logical_or(odd, t == 4), sixth[half:], sixth[:half])

        if far:
            when(is_dst, jnp.logical_not(far_dst_first))(add_moved)
        chunk[...] = total[...].astype(BF16)
        gathered[t] = chunk[...]
        for j in range(adders):

            @when(j != t)
            def _():
                ag_copy(j, t).start()

    if far:

        @when(rank < n_t - 1)
        def _():
            pl.semaphore_wait(here.at[n_t - 1], 1)

        @when(t < adders)
        def _():
            ag_copy(n_t - 1, t).start()

    for c in range(adders):

        @when(t != c)
        def _():
            ag_copy(0, c).wait_recv()

    for c in range(10):
        for k in range(2):
            for h in range(2):
                n, m = home_of(c, k, h)
                out[h * half : (h + 1) * half, (2 * c + k) * LANES : (2 * c + k + 1) * LANES] = (
                    gathered[n, m]
                )

    if far:

        @when(adds)
        def _():
            for j in range(n_t):
                far_copy(j).wait_recv()
            arrived = far_in[0].astype(F32)
            for j in range(1, n_t):
                arrived = arrived + far_in[j].astype(F32)
            far_row[...] = jnp.where(has_arrival, arrived, 0.0).astype(BF16)

        @when(far_dst_first, jnp.logical_not(adds))
        def _():
            row_copy(0).wait_recv()

        for spot, followers in tree.items():

            @when(far_dst_first, my_place == spot)
            def _():
                for j in followers:
                    row_copy(place_in_tree(j)).start()

        @when(far_dst_first)
        def _():
            for c in range(10):
                pair = jnp.concatenate([far_row[c, :steps], far_row[c, steps:]], axis=1)
                out[:, 256 * c : 256 * (c + 1)] += dot(place, pair).astype(BF16)

        for spot, followers in tree.items():

            @when(far_dst_first, my_place == spot)
            def _():
                for j in followers:
                    row_copy(place_in_tree(j)).wait_send()

    for j in range(n_t):

        @when(t != j, t < adders)
        def _():
            ag_copy(j, t).wait_send()

    for c in range(adders):

        @when(t != c)
        def _():
            rs_copy(c, t).wait_send()

    if far:

        @when(far_src_last)
        def _():
            far_copy(t).wait_send()

        @when(is_src, jnp.logical_not(far_src_last))
        def _():
            for c in range(adders):
                mv_copy(c, t).wait_send()

    else:

        @when(is_src)
        def _():
            back_copy(up).wait_send()

    @pl.when(is_dst)
    def _():
        ask_copy(down, t).wait_send()

    if far:

        @pl.when(relays)
        def _():
            for j in range(n_t):
                pass_copy(j).wait_send()


def parity_kernel(mig_hbm, out, mig, sem):
    load = pltpu.make_async_copy(mig_hbm, mig, sem)
    load.start()
    load.wait()
    out[0] = lax.rem(mig[0, 0], 2)


def source_parity(moves):
    return pl.pallas_call(
        parity_kernel,
        out_shape=jax.ShapeDtypeStruct((1,), jnp.int32),
        in_specs=[pl.BlockSpec(memory_space=pltpu.HBM)],
        out_specs=pl.BlockSpec(memory_space=pltpu.SMEM),
        scratch_shapes=[pltpu.SMEM(moves.shape, jnp.int32), pltpu.SemaphoreType.DMA],
    )(moves)[0]


def project(parity, n_dp, n_t, *operands):
    lengths, finished, moves, queries, new_keys, new_values, keys, values, weight = operands
    steps, slots, width = queries.shape
    features = weight.shape[1]
    heads = width // HD
    rows = steps * slots
    dma = pltpu.SemaphoreType.DMA
    regular = pltpu.SemaphoreType.REGULAR
    asks = ((heads + 2) * steps, HD)
    pieces = (n_t, 6 if parity else 5, rows // 2, LANES)
    parts = (n_t - 1 if parity else n_t,) + pieces[1:]
    moved = (n_t, 3, 2 * steps, LANES)
    moved_parts = (n_t - 1,) + moved[1:]
    far = (features // (2 * LANES), 2 * steps, LANES)
    return pl.pallas_call(
        functools.partial(
            kernel, slots=slots, steps=steps, heads=heads, n_dp=n_dp, n_t=n_t, parity=parity
        ),
        out_shape=jax.ShapeDtypeStruct((rows, features), BF16),
        in_specs=[pl.BlockSpec(memory_space=pltpu.HBM)] * 9,
        out_specs=pl.BlockSpec(memory_space=pltpu.VMEM),
        scratch_shapes=[
            pltpu.SMEM(lengths.shape, jnp.int32),
            pltpu.SMEM(finished.shape, jnp.int32),
            pltpu.VMEM(moves.shape, jnp.int32),
            pltpu.VMEM(queries.shape, BF16),
            pltpu.VMEM(new_keys.shape, BF16),
            pltpu.VMEM(new_values.shape, BF16),
            pltpu.VMEM(keys.shape, BF16),
            pltpu.VMEM(values.shape, BF16),
            pltpu.VMEM(weight.shape, BF16),
            pltpu.VMEM(asks, BF16),
            pltpu.VMEM(asks, BF16),
            pltpu.VMEM((n_t,) + asks, BF16),
            pltpu.VMEM(parts, BF16),
            pltpu.VMEM(pieces, BF16),
            pltpu.VMEM(moved_parts, BF16),
            pltpu.VMEM(moved, BF16),
            pltpu.VMEM(far, BF16),
            pltpu.VMEM((n_t,) + far, BF16),
            pltpu.VMEM(far, BF16),
            pltpu.VMEM((heads * steps, HD), BF16),
            pltpu.VMEM((heads * steps, HD), BF16),
            pltpu.VMEM((rows, width), F32),
            pltpu.VMEM(pieces[1:], F32),
            pltpu.VMEM(pieces[1:], BF16),
            pltpu.VMEM(parts, BF16),
            dma((6 + 2 * slots + 10,)), dma, dma, dma((n_t,)), dma((n_t,)),
            dma((n_t,)), dma((n_t,)), dma((n_t,)), dma((n_t,)), dma((n_t,)), dma((n_t,)),
            dma, dma((n_t,)), dma((n_t,)), dma, dma, dma,
            regular((n_t,)), regular((n_t,)), regular((n_t,)),
        ],
        compiler_params=pltpu.CompilerParams(
            collective_id=parity, has_side_effects=True, vmem_limit_bytes=48 << 20
        ),
    )(*operands)


def per_device(n_dp, n_t, cache_keys, cache_values, lengths, finished, migrations, queries,
               new_keys, new_values, out_weight):
    steps, slots, _ = queries.shape
    moves = migrations.T
    result = lax.cond(
        source_parity(moves) == 0,
        functools.partial(project, 0, n_dp, n_t),
        functools.partial(project, 1, n_dp, n_t),
        lengths, finished, moves, queries, new_keys, new_values,
        cache_keys, cache_values, out_weight,
    )
    return result.reshape(steps, slots, out_weight.shape[1])


def solution(mesh):
    sizes = dict(zip(mesh.axis_names, mesh.devices.shape))
    return jax.shard_map(
        functools.partial(per_device, sizes["dp"], sizes["tensor"]),
        mesh=mesh,
        in_specs=(
            P("dp", None, "tensor"),
            P("dp", None, "tensor"),
            P("dp"),
            P("dp"),
            P(),
            P(None, "dp", "tensor"),
            P(None, "dp", "tensor"),
            P(None, "dp", "tensor"),
            P("tensor", None),
        ),
        out_specs=P(None, "dp", None),
        check_vma=False,
    )
```
